128 devices in a mesh: blk: 16 (over y_hi, x, core), hid: 8 (over y_lo, z).
Axes of the slice: x: 4, y: 4 (y_hi: 2, y_lo: 2; y = y_hi * 2 + y_lo), z: 4, core: 2. Of those that a mesh axis runs over, the one named last changes fastest.
Arguments:
- hyp_emb: bfloat16 [256, 1024], P('blk'), may hold values from -6 to 6
- ref_emb: bfloat16 [256, 1024], P('blk'), may hold values from -6 to 6
- hyp_part: bfloat16 [256, 3072], P('blk', 'hid'), may hold values from -4 to 4
- ref_part: bfloat16 [256, 3072], P('blk', 'hid'), may hold values from -4 to 4
- pair_weight: bfloat16 [2048, 3072], P(None, 'hid'), may hold values from -0.125 to 0.125
- out_weight: bfloat16 [3072, 1024], P('hid'), may hold values from -0.21875 to 0.21875
- out_bias: float32 [1024], P('hid'), may hold values from -4 to 4
- score_weight: float32 [1024], P('hid'), may hold values from -0.04 to 0.04
Outputs:
- scores: float32 [256, 256], P('blk')
- utilities: float32 [256], P('blk')
The draws below stay inside these ranges and needn't reach their ends.
All inputs are finite; a program needn't handle non-finite values.
Results may differ from the reference program's by a relative error of at most 0.013.
Values may be sent and summed in bfloat16 or wider, within the bound.
A program may use at most 64 MiB of HBM per device.

```python
import jax
import jax.numpy as jnp
from jax import lax

D = 1024
HID1 = 3072
HID2 = 1024
HYPS = 256
REFS = 256
N_HID = 8


def draw_score_weight(key, part):
    key = jax.random.fold_in(key, 11)
    sign_key, size_key = jax.random.split(key)
    signs = (2 * jax.random.randint(sign_key, (HID2,), 0, 2) - 1).astype(jnp.float32)
    magnitude = jax.random.uniform(size_key, (HID2,), jnp.float32, 0.025, 0.04)
    return (signs * magnitude).astype(jnp.float32)


def block_levels(own_key, shape, cuts, least, top_value):
    def one(position, shards_of):
        draws = jax.random.uniform(jax.random.fold_in(jax.random.fold_in(own_key, 6), position), (shards_of,), jnp.float32, least / len(cuts), top_value / len(cuts))
        return jnp.repeat(jnp.exp(draws), shape[position] // shards_of).reshape((-1,) + (1,) * (len(shape) - position - 1))

    level = one(*cuts[0])
    for cut in cuts[1:]:
        level = level * one(*cut)
    return level


def normal_values(stream_key, extent, spread, reach, cuts=(), held_as=jnp.bfloat16):
    values = spread * jax.random.normal(stream_key, extent, jnp.float32)
    if cuts:
        values = values * block_levels(stream_key, extent, cuts, -0.22, 0.18)
    return jnp.clip(values, -reach, reach).astype(held_as)


def setup_inputs(seed: int = 0) -> dict:
    arg_keys = jax.random.split(jax.random.key(seed), 9)
    return {
        "hyp_emb": normal_values(arg_keys[0], (HYPS, D), 1.0, 6.0, ((0, 16),)),
        "ref_emb": normal_values(arg_keys[1], (REFS, D), 1.0, 6.0, ((0, 16),)),
        "hyp_part": normal_values(arg_keys[2], (HYPS, HID1), 0.5, 4.0, ((0, 16), (1, 8))),
        "ref_part": normal_values(arg_keys[3], (REFS, HID1), 0.5, 4.0, ((0, 16), (1, 8))),
        "pair_weight": normal_values(arg_keys[4], (2 * D, HID1), (2 * D) ** -0.5, 0.125, ((1, 8),)),
        "out_weight": normal_values(arg_keys[5], (HID1, HID2), (HID1 // 4) ** -0.5, 0.21875, ((0, 8),)),
        "out_bias": normal_values(arg_keys[6], (HID2,), 0.5, 4.0, ((0, 8),), jnp.float32),
        "score_weight": draw_score_weight(jax.random.fold_in(arg_keys[8], 71), 0),
    }


def reference(hyp_emb, ref_emb, hyp_part, ref_part, pair_weight, out_weight, out_bias, score_weight):
    group = HID1 // N_HID
    blocks_emb = hyp_emb.reshape(HYPS // 8, 8, D)
    blocks_part = hyp_part.reshape(HYPS // 8, 8, HID1)

    def one_block(pieces):
        block_emb, block_part = pieces
        left = block_emb.astype(jnp.float32)[:, None, :]
        right = ref_emb.astype(jnp.float32)[None, :, :]
        prod = (left * right).astype(jnp.bfloat16).reshape(8 * REFS, D)
        diff = jnp.abs(left - right).astype(jnp.bfloat16).reshape(8 * REFS, D)
        feats = jnp.concatenate([prod, diff], axis=1)
        inner = jnp.dot(feats, pair_weight, preferred_element_type=jnp.float32).reshape(8, REFS, HID1)
        inner = inner + block_part.astype(jnp.float32)[:, None, :] + ref_part.astype(jnp.float32)[None, :, :]
        first = jnp.tanh(inner).astype(jnp.bfloat16).reshape(8 * REFS, HID1)
        total = jnp.zeros((8 * REFS, HID2), jnp.float32)
        for index in range(N_HID):
            piece = jnp.dot(first[:, index * group:(index + 1) * group], out_weight[index * group:(index + 1) * group], preferred_element_type=jnp.float32)
            piece = lax.optimization_barrier(piece.astype(jnp.bfloat16))
            total = total + piece.astype(jnp.float32)
        second = jnp.tanh(total + out_bias[None, :])
        return jnp.dot(second, score_weight, precision=lax.Precision.HIGHEST).reshape(8, REFS)

    scores = lax.map(one_block, (blocks_emb, blocks_part)).reshape(HYPS, REFS)
    utilities = jnp.mean(scores, axis=1)
    return scores, utilities
```

```python
import functools

import jax
import jax.numpy as jnp
from jax import lax
from jax.experimental import pallas as pl
from jax.experimental.pallas import tpu as pltpu
from jax.sharding import PartitionSpec as P

MESH = pl.DeviceIdType.MESH
BF16 = jnp.bfloat16
F32 = jnp.float32

STEPS1 = 8
STEPS2 = 4
STEPS = STEPS1 + STEPS2
K1 = 2048 // STEPS1
Q1 = K1 // 4
C2 = 1024 // STEPS2
U = 384
AHEAD = 3


def mod(a, n):
    return lax.rem(a, jnp.int32(n))


def half(a):
    return lax.div(a, jnp.int32(2))


def device(x, y, z, c):
    return ((half(y) * 4 + x) * 2 + c, mod(y, 2) * 4 + z)


def slot_of(rel):
    return rel + half(rel) * (5 - 2 * rel)


SLOT_AT = {0: 0, 1: 2, 2: 3, 3: 1}


def kernel(
    hyp_emb, ref_emb, hyp_part, ref_part, w1_in, w2_in, bias_in, score_in,
    scores_out, util_out,
    w1, w2, hyp, ref, hp, rp, bs, feats, acc, first, part_send, part_recv, part_mine, sc, sm,
    hypf, hpf, rpf, sacc,
    z_recv, x_recv, d_recv, z_send, x_send, d_send,
    small_recv, hp_send, rp_send, ref_send, bs_send, loc, pr_recv, pr_send, sc_send,
):
    blk = lax.axis_index("blk")
    hid = lax.axis_index("hid")
    c = mod(blk, 2)
    x = mod(half(blk), 4)
    y_hi = lax.div(blk, jnp.int32(8))
    y_lo = lax.div(hid, jnp.int32(4))
    y = y_hi * 2 + y_lo
    z = mod(hid, 4)

    def zz(d):
        return mod(z + d, 4)

    def yy(d):
        return mod(y + d, 4)

    def xx(d):
        return mod(x + d, 4)

    sibling = device(x, y, z, 1 - c)
    z_up, z_down = device(x, y, zz(1), c), device(x, y, zz(3), c)
    x_up, x_down = device(xx(1), y, z, c), device(xx(3), y, z, c)

    ref_j = mod(c + y_lo, 2)
    ref_y = mod(y + 2 * c * (1 - y_lo), 4)
    ref_self = jnp.logical_and(ref_y == y, x == z)

    barrier = pltpu.get_barrier_semaphore()

    def greet(target):
        pl.semaphore_signal(barrier, inc=1, device_id=target, device_id_type=MESH)

    for dy in range(4):
        for dz in range(4):
            if dy or dz:
                greet(device(x, yy(dy), zz(dz), c))
    greet(sibling)
    greet(x_up)
    greet(x_down)
    for j in range(2):
        e = yy(4 - j)
        src_y = half(e) * 2 + y_lo
        src_c = mod(e, 2)
        for dz in range(4):
            is_me = (
                jnp.logical_and(jnp.logical_and(src_y == y, src_c == c), x == z) if dz == 0 else None
            )
            target = device(z, src_y, zz(dz), src_c)
            if is_me is None:
                greet(target)
            else:
                pl.when(jnp.logical_not(is_me))(functools.partial(greet, target))
    pl.semaphore_wait(barrier, 15 + 3 + 8 - jnp.where(ref_self, 1, 0))

    def remote(src, dst, send, recv, target):
        pltpu.make_async_remote_copy(
            src_ref=src, dst_ref=dst, send_sem=send, recv_sem=recv, device_id=target, device_id_type=MESH
        ).start()

    def local(src, dst, sem):
        pltpu.make_async_copy(src, dst, sem).start()

    def done(region, sem):
        pltpu.make_async_copy(region, region, sem).wait()

    quarter = mod(x, 2) * 2 + c
    quarter_x = (1 - mod(x, 2)) * 2 + c

    def region(t, quarter_, slots):
        lo, n = slots
        if t < STEPS1:
            rows = pl.ds(pl.multiple_of(t * K1 + quarter_ * Q1, Q1), Q1)
            return w1.at[rows, pl.ds(lo * U, n * U)]
        rows = pl.ds(pl.multiple_of(quarter_ * 96, 96), 96)
        return w2.at[pl.ds(lo, n), rows, pl.ds((t - STEPS1) * C2, C2)]

    def own_piece(t):
        if t < STEPS1:
            rows = pl.ds(pl.multiple_of(t * K1 + quarter * Q1, Q1), Q1)
            return w1_in.at[rows, :]
        rows = pl.ds(pl.multiple_of(quarter * 96, 96), 96)
        return w2_in.at[:, rows, pl.ds((t - STEPS1) * C2, C2)]

    def send_own(t):
        remote(own_piece(t), region(t, quarter, (1, 1)), z_send.at[0, t], z_recv.at[0, t], z_down)
        remote(own_piece(t), region(t, quarter, (2, 1)), z_send.at[1, t], z_recv.at[1, t], z_up)

    local(hyp_emb, hyp.at[0], small_recv.at[0])
    remote(hyp_emb, hyp.at[1], loc.at[3], small_recv.at[0], device(x, yy(2), z, c))

    def send_refs():
        for k in range(8):
            dx, dc = k // 2, k % 2
            target = device(xx(dx), ref_y, z, mod(c + dc, 2))
            if k == 0:
                pl.when(ref_self)(lambda: local(ref_emb, ref.at[ref_j], small_recv.at[1]))
                pl.when(jnp.logical_not(ref_self))(
                    lambda: remote(ref_emb, ref.at[ref_j], ref_send.at[k], small_recv.at[1], target)
                )
            else:
                remote(ref_emb, ref.at[ref_j], ref_send.at[k], small_recv.at[1], target)

    pl.when(x == z)(send_refs)
    send_own(0)
    local(w1_in, w1.at[:, pl.ds(0, U)], loc.at[0])
    local(w2_in, w2.at[pl.ds(0, 1)], loc.at[1])
    local(hyp_part, hp.at[0, 0], small_recv.at[2])
    for d in range(1, 4):
        remote(hyp_part, hp.at[0, SLOT_AT[d]], hp_send.at[d], small_recv.at[2], device(x, y, zz(d), c))
    for d in range(4):
        remote(hyp_part, hp.at[1, SLOT_AT[d]], hp_send.at[4 + d], small_recv.at[2], device(x, yy(2), zz(d), c))
    ref_slot = slot_of(mod(z - x + 4, 4))
    for k in range(8):
        dx, dc = k // 2, k % 2
        target = device(xx(dx), ref_y, x, mod(c + dc, 2))
        there = rp.at[ref_j, ref_slot]
        if k == 0:
            pl.when(ref_self)(lambda: local(ref_part, there, small_recv.at[3]))
            pl.when(jnp.logical_not(ref_self))(
                lambda: remote(ref_part, there, rp_send.at[k], small_recv.at[3], target)
            )
        else:
            remote(ref_part, there, rp_send.at[k], small_recv.at[3], target)
    for t in range(1, AHEAD):
        send_own(t)
    bs[hid] = jnp.concatenate([bias_in[...], score_in[...], jnp.zeros((6, 128), F32)], axis=0)
    for d in range(1, 8):
        remote(bs.at[hid], bs.at[hid], bs_send.at[d], small_recv.at[4], (blk, mod(hid + d, 8)))

    def forward_z(t):
        done(region(t, quarter, (1, 1)), z_recv.at[0, t])
        done(region(t, quarter, (2, 1)), z_recv.at[1, t])
        if t % 2 == 0:
            remote(region(t, quarter, (1, 1)), region(t, quarter, (3, 1)), z_send.at[2, t], z_recv.at[2, t], z_down)
        else:
            remote(region(t, quarter, (2, 1)), region(t, quarter, (3, 1)), z_send.at[2, t], z_recv.at[2, t], z_up)
        two = region(t, quarter, (1, 2))
        remote(two, two, x_send.at[0, t], x_recv.at[0, t], x_up if t % 2 == 0 else x_down)
        if t + AHEAD < STEPS:
            send_own(t + AHEAD)
        remote(two, two, d_send.at[0, t], d_recv.at[0, t], sibling)

    def forward_z3(t):
        one = region(t, quarter, (3, 1))
        done(one, z_recv.at[2, t])
        remote(one, one, x_send.at[1, t], x_recv.at[1, t], x_up if t % 2 == 0 else x_down)
        remote(one, one, d_send.at[1, t], d_recv.at[1, t], sibling)

    def forward_x(t):
        two = region(t, quarter_x, (1, 2))
        done(two, x_recv.at[0, t])
        remote(two, two, d_send.at[2, t], d_recv.at[2, t], sibling)

    def forward_x3(t):
        one = region(t, quarter_x, (3, 1))
        done(one, x_recv.at[1, t])
        remote(one, one, d_send.at[3, t], d_recv.at[3, t], sibling)

    def arrived(t):
        other, other_x = quarter + 1 - 2 * c, quarter_x + 1 - 2 * c
        done(region(t, other, (1, 2)), d_recv.at[0, t])
        done(region(t, other, (3, 1)), d_recv.at[1, t])
        done(region(t, other_x, (1, 2)), d_recv.at[2, t])
        done(region(t, other_x, (3, 1)), d_recv.at[3, t])

    def drain(t):
        done(own_piece(t), z_send.at[0, t])
        done(own_piece(t), z_send.at[1, t])
        one, two = region(t, quarter, (3, 1)), region(t, quarter, (1, 2))
        done(one, z_send.at[2, t])
        done(two, x_send.at[0, t])
        done(one, x_send.at[1, t])
        done(two, d_send.at[0, t])
        done(one, d_send.at[1, t])
        done(two, d_send.at[2, t])
        done(one, d_send.at[3, t])

    def make_feats():
        done(hyp, small_recv.at[0])
        done(ref, small_recv.at[1])
        hypf[...] = hyp[...].astype(F32).reshape(32, 1024)
        right = [ref[j].astype(F32) for j in range(2)]

        def one(h, carry):
            left = hypf[pl.ds(h, 1), :]
            for j in range(2):
                rows = pl.ds(pl.multiple_of(j * 512 + h * 16, 16), 16)
                feats[rows, pl.ds(0, 1024)] = (left * right[j]).astype(BF16)
                feats[rows, pl.ds(1024, 1024)] = jnp.abs(left - right[j]).astype(BF16)
            return carry

        lax.fori_loop(0, 32, one, 0)

    def multiply(k, depth, begin):
        def block(i, carry):
            rows = pl.ds(pl.multiple_of(i * 256, 256), 256)
            left = feats[rows, pl.ds(k, depth)]
            for n in range(3):
                columns = pl.ds(n * 512, 512)
                value = jnp.dot(left, w1[pl.ds(k, depth), columns], preferred_element_type=F32)
                if not begin:
                    value = acc[rows, columns] + value
                acc[rows, columns] = value
            return carry

        lax.fori_loop(0, 4, block, 0)

    def make_parts():
        done(hp, small_recv.at[2])
        done(rp, small_recv.at[3])
        for s in range(2):
            for g in range(4):
                hpf[s, :, pl.ds(g * U, U)] = hp[s, g].astype(F32)
                rpf[s, :, pl.ds(g * U, U)] = rp[s, g].astype(F32)

    mine = mod(y_hi + y_lo, 2)

    def finish_first(k, depth):
        def block(i, carry):
            edge = mod(i, 2)
            slot = jnp.where(i < 2, 1 - mine, mine)
            base = pl.multiple_of(edge * 512 + slot * 256, 256)
            rows = pl.ds(base, 256)
            left = feats[rows, pl.ds(k, depth)]
            for n in range(3):
                columns = pl.ds(n * 512, 512)
                acc[rows, columns] += jnp.dot(left, w1[pl.ds(k, depth), columns], preferred_element_type=F32)

            def one(h, carry):
                here = pl.ds(pl.multiple_of(base + h * 16, 16), 16)
                there = pl.ds(pl.multiple_of(i * 256 + h * 16, 16), 16)
                value = acc[here, :] + hpf[slot, pl.ds(h, 1), :] + rpf[edge]
                first[there, :] = jnp.tanh(value).astype(BF16)
                return carry

            lax.fori_loop(0, 16, one, 0)
            return carry

        lax.fori_loop(0, 4, block, 0)

    def second_weights(n):
        return w2[:, :, pl.ds(n * C2, C2)].reshape(4 * U, C2)

    def theirs(n):
        columns = pl.ds(n * C2, C2)
        for j in range(2):
            value = jnp.dot(first[pl.ds(j * 256, 256), :], second_weights(n), preferred_element_type=F32)
            part_send[j, :, columns] = value.astype(BF16)
            remote(
                part_send.at[j, :, columns], part_recv.at[1 - j, :, columns], pr_send.at[j, n], pr_recv.at[1 - j, n],
                device(x, yy(1) if j == 0 else yy(3), z, c),
            )

    def ours(n):
        for j in range(2):
            part_mine[j, :, pl.ds(n * C2, C2)] = jnp.dot(
                first[pl.ds(512 + j * 256, 256), :], second_weights(n), preferred_element_type=F32
            )

    def finish_second(n):
        columns = pl.ds(n * C2, C2)
        for j in range(2):
            done(part_recv.at[j, :, columns], pr_recv.at[j, n])
            total = jnp.zeros((256, 128), F32) if n == 0 else sacc[j]
            for k in range(C2 // 128):
                g = n * (C2 // 128) + k
                lanes = pl.ds(g * 128, 128)
                value = part_mine[j, :, lanes] + part_recv[j, :, lanes].astype(F32)
                total += jnp.tanh(value + bs[g, 0:1, :]) * bs[g, 1:2, :]
            sacc[j] = total

    for t in range(STEPS + 3):
        if t < STEPS:
            forward_z(t)
        if 0 <= t - 1 < STEPS:
            forward_z3(t - 1)
            forward_x(t - 1)
        if 0 <= t - 2 < STEPS:
            forward_x3(t - 2)
        if t == 1:
            make_feats()
        if t == 2:
            make_parts()
            done(w1_in, loc.at[0])
            done(w2_in, loc.at[1])
        a = t - 3
        if 0 <= a:
            arrived(a)
        if a in (1, 3, 5):
            multiply((a - 1) * K1, 2 * K1, a == 1)
        if a == 7:
            finish_first(6 * K1, 2 * K1)
        if a >= STEPS1:
            theirs(a - STEPS1)
            ours(a - STEPS1)
    done(bs.at[pl.ds(0, 7)], small_recv.at[4])
    for n in range(STEPS2):
        finish_second(n)

    lane = lax.broadcasted_iota(jnp.int32, (256, 128), 1)
    row = lax.broadcasted_iota(jnp.int32, (256, 128), 0)
    sums = [jnp.zeros((16, 128), F32), jnp.zeros((16, 128), F32)]
    for j in range(2):
        e = yy(4 - j)
        place = z * 32 + mod(e, 2) * 16
        value = jnp.sum(sacc[j], axis=1, keepdims=True)
        value = jnp.where(lane - place == jnp.bitwise_and(row, 15), value, 0.0)
        value = jnp.sum(value.reshape(16, 16, 128), axis=1)
        for k in range(2):
            sums[k] += jnp.where(half(e) == k, value, 0.0)
    sm[:, pl.ds(0, 128)] = sums[0]
    sm[:, pl.ds(128, 128)] = sums[1]

    sc_row = y_hi * 4 + z
    sc_self = mod(y, 2) == y_hi
    for d in range(8):
        target = (mod(y, 2) * 8 + mod(blk, 8), mod(hid + d, 8))
        if d == 0:
            pl.when(sc_self)(lambda: local(sm, sc.at[sc_row], small_recv.at[5]))
            pl.when(jnp.logical_not(sc_self))(
                lambda: remote(sm, sc.at[sc_row], sc_send.at[d], small_recv.at[5], target)
            )
        else:
            remote(sm, sc.at[sc_row], sc_send.at[d], small_recv.at[5], target)

    for t in range(STEPS):
        drain(t)
    done(hyp_emb, loc.at[3])
    for d in range(1, 8):
        done(hyp_part, hp_send.at[d])
        done(bs.at[0], bs_send.at[d])
    for k in range(8):
        if k == 0:
            pl.when(jnp.logical_and(x == z, jnp.logical_not(ref_self)))(lambda: done(ref_emb, ref_send.at[0]))
            pl.when(jnp.logical_not(ref_self))(lambda: done(ref_part, rp_send.at[0]))
        else:
            pl.when(x == z)(lambda: done(ref_emb, ref_send.at[k]))
            done(ref_part, rp_send.at[k])
    for j in range(2):
        for n in range(STEPS2):
            done(part_send.at[j, :, pl.ds(n * C2, C2)], pr_send.at[j, n])

    done(sc, small_recv.at[5])
    total = sc[0]
    for k in range(1, 8):
        total += sc[k]
    scores_out[...] = total
    mean = jnp.sum(total, axis=1, keepdims=True) * (1.0 / 256.0)
    lane = lax.broadcasted_iota(jnp.int32, (16, 128), 1)
    row = lax.broadcasted_iota(jnp.int32, (16, 128), 0)
    spread = jnp.sum(jnp.where(lane == row, mean, 0.0), axis=0, keepdims=True)
    util_out[...] = spread[:, :16]

    for d in range(8):
        if d == 0:
            pl.when(jnp.logical_not(sc_self))(lambda: done(sm, sc_send.at[0]))
        else:
            done(sm, sc_send.at[d])


def body(hyp_emb, ref_emb, hyp_part, ref_part, pair_weight, out_weight, out_bias, score_weight):
    any_space = pl.BlockSpec(memory_space=pl.ANY)
    vmem = pl.BlockSpec(memory_space=pltpu.VMEM)
    dma = pltpu.SemaphoreType.DMA
    scores, utilities = pl.pallas_call(
        kernel,
        out_shape=(jax.ShapeDtypeStruct((16, 256), F32), jax.ShapeDtypeStruct((1, 16), F32)),
        in_specs=[any_space] * 6 + [vmem] * 2,
        out_specs=(vmem, vmem),
        scratch_shapes=[
            pltpu.VMEM((2048, 4 * U), BF16),
            pltpu.VMEM((4, U, 1024), BF16),
            pltpu.VMEM((2, 16, 1024), BF16),
            pltpu.VMEM((2, 16, 1024), BF16),
            pltpu.VMEM((2, 4, 16, U), BF16),
            pltpu.VMEM((2, 4, 16, U), BF16),
            pltpu.VMEM((8, 8, 128), F32),
            pltpu.VMEM((1024, 2048), BF16),
            pltpu.VMEM((1024, 4 * U), F32),
            pltpu.VMEM((1024, 4 * U), BF16),
            pltpu.VMEM((2, 256, 1024), BF16),
            pltpu.VMEM((2, 256, 1024), BF16),
            pltpu.VMEM((2, 256, 1024), F32),
            pltpu.VMEM((8, 16, 256), F32),
            pltpu.VMEM((16, 256), F32),
            pltpu.VMEM((32, 1024), F32),
            pltpu.VMEM((2, 16, 4 * U), F32),
            pltpu.VMEM((2, 16, 4 * U), F32),
            pltpu.VMEM((2, 256, 128), F32),
            dma((3, STEPS)), dma((2, STEPS)), dma((4, STEPS)),
            dma((3, STEPS)), dma((2, STEPS)), dma((4, STEPS)),
            dma((6,)), dma((8,)), dma((8,)), dma((8,)), dma((8,)), dma((4,)),
            dma((2, STEPS2)), dma((2, STEPS2)), dma((8,)),
        ],
        compiler_params=pltpu.CompilerParams(
            collective_id=0, has_side_effects=True, vmem_limit_bytes=50 * 2**20
        ),
        cost_estimate=pl.CostEstimate(flops=9_663_676_416, bytes_accessed=3_000_000, transcendentals=2_097_152),
        name="mbr_scores",
    )(
        hyp_emb, ref_emb, hyp_part, ref_part, pair_weight, out_weight.reshape(1, U, 1024),
        out_bias.reshape(1, 128), score_weight.reshape(1, 128),
    )
    return scores, utilities.reshape(16)


def solution(mesh):
    in_specs = (
        P("blk", None),
        P("blk", None),
        P("blk", "hid"),
        P("blk", "hid"),
        P(None, "hid"),
        P("hid", None),
        P("hid"),
        P("hid"),
    )
    out_specs = (P("blk", None), P("blk"))
    return jax.shard_map(body, mesh=mesh, in_specs=in_specs, out_specs=out_specs, check_vma=False)
```

```python
import functools

import jax
import jax.numpy as jnp
from jax import lax
from jax.experimental import pallas as pl
from jax.experimental.pallas import tpu as pltpu
from jax.sharding import PartitionSpec as P

MESH = pl.DeviceIdType.MESH
BF16 = jnp.bfloat16
F32 = jnp.float32

STEPS1 = 8
STEPS2 = 4
STEPS = STEPS1 + STEPS2
K1 = 2048 // STEPS1
Q1 = K1 // 4
C2 = 1024 // STEPS2
U = 384
AHEAD = 2
LZ3, LX, LX3, L12, L3 = 2, 2, 4, 3, 5


def mod(a, n):
    return lax.rem(a, jnp.int32(n))


def half(a):
    return lax.div(a, jnp.int32(2))


def device(x, y, z, c):
    return ((half(y) * 4 + x) * 2 + c, mod(y, 2) * 4 + z)


def slot_of(rel):
    return rel + half(rel) * (5 - 2 * rel)


SLOT_AT = {0: 0, 1: 2, 2: 3, 3: 1}


def kernel(
    hyp_emb, ref_emb, hyp_part, ref_part, w1_in, w2_in, bias_in, score_in,
    scores_out, util_out,
    w1, w2, hyp, ref, hp, rp, bs, my_bs, feats, acc, first, part_send, part_recv, part_mine, sc, sm,
    hypf, hpf, rpf, sacc,
    z_recv, z3_recv, x_recv, x3_recv, d_recv, d3_recv, w_send, small_recv, small_send, loc, pr_recv,
):
    blk = lax.axis_index("blk")
    hid = lax.axis_index("hid")
    c = mod(blk, 2)
    x = mod(half(blk), 4)
    y_hi = lax.div(blk, jnp.int32(8))
    y_lo = lax.div(hid, jnp.int32(4))
    y = y_hi * 2 + y_lo
    z = mod(hid, 4)

    def zz(d):
        return mod(z + d, 4)

    def yy(d):
        return mod(y + d, 4)

    def xx(d):
        return mod(x + d, 4)

    sibling = device(x, y, z, 1 - c)
    z_up, z_down = device(x, y, zz(1), c), device(x, y, zz(3), c)
    x_up, x_down = device(xx(1), y, z, c), device(xx(3), y, z, c)

    ref_j = mod(c + y_lo, 2)
    ref_y = mod(y + 2 * c * (1 - y_lo), 4)
    ref_self = jnp.logical_and(ref_y == y, x == z)

    barrier = pltpu.get_barrier_semaphore()

    def greet(target):
        pl.semaphore_signal(barrier, inc=1, device_id=target, device_id_type=MESH)

    for dy in range(4):
        for dz in range(4):
            if dy or dz:
                greet(device(x, yy(dy), zz(dz), c))
    greet(sibling)
    greet(x_up)
    greet(x_down)
    for j in range(2):
        e = yy(4 - j)
        src_y = half(e) * 2 + y_lo
        src_c = mod(e, 2)
        for dz in range(4):
            is_me = (
                jnp.logical_and(jnp.logical_and(src_y == y, src_c == c), x == z) if dz == 0 else None
            )
            target = device(z, src_y, zz(dz), src_c)
            if is_me is None:
                greet(target)
            else:
                pl.when(jnp.logical_not(is_me))(functools.partial(greet, target))
    pl.semaphore_wait(barrier, 15 + 3 + 8 - jnp.where(ref_self, 1, 0))

    def remote(src, dst, send, recv, target):
        pltpu.make_async_remote_copy(
            src_ref=src, dst_ref=dst, send_sem=send, recv_sem=recv, device_id=target, device_id_type=MESH
        ).start()

    def local(src, dst, sem):
        pltpu.make_async_copy(src, dst, sem).start()

    def done(region, sem):
        pltpu.make_async_copy(region, region, sem).wait()

    quarter = mod(x, 2) * 2 + c
    quarter_x = (1 - mod(x, 2)) * 2 + c

    def region(t, quarter_, slots, part=None):
        lo, n = slots
        size = Q1 if t < STEPS1 else 96
        first_row = quarter_ * size
        if part is not None:
            size //= 2
            first_row += part * size
        if t < STEPS1:
            rows = pl.ds(pl.multiple_of(t * K1 + first_row, size), size)
            return w1.at[rows, pl.ds(lo * U, n * U)]
        rows = pl.ds(pl.multiple_of(first_row, size), size)
        return w2.at[pl.ds(lo, n), rows, pl.ds((t - STEPS1) * C2, C2)]

    def own_piece(t):
        if t < STEPS1:
            rows = pl.ds(pl.multiple_of(t * K1 + quarter * Q1, Q1), Q1)
            return w1_in.at[rows, :]
        rows = pl.ds(pl.multiple_of(quarter * 96, 96), 96)
        return w2_in.at[:, rows, pl.ds((t - STEPS1) * C2, C2)]

    def send(src, dst, recv, target, t):
        remote(src, dst, w_send.at[0 if t < STEPS1 else 1], recv, target)

    def send_own(t):
        send(own_piece(t), region(t, quarter, (1, 1)), z_recv.at[t], z_down, t)
        send(own_piece(t), region(t, quarter, (2, 1)), z_recv.at[t], z_up, t)

    local(hyp_emb, hyp.at[0], small_recv.at[0])
    remote(hyp_emb, hyp.at[1], small_send.at[0], small_recv.at[0], device(x, yy(2), z, c))

    def send_refs():
        for k in range(8):
            dx, dc = k // 2, k % 2
            target = device(xx(dx), ref_y, z, mod(c + dc, 2))
            if k == 0:
                pl.when(ref_self)(lambda: local(ref_emb, ref.at[ref_j], small_recv.at[1]))
                pl.when(jnp.logical_not(ref_self))(
                    lambda: remote(ref_emb, ref.at[ref_j], small_send.at[1], small_recv.at[1], target)
                )
            else:
                remote(ref_emb, ref.at[ref_j], small_send.at[1], small_recv.at[1], target)

    for t in range(AHEAD):
        send_own(t)
    pl.when(x == z)(send_refs)
    local(w1_in, w1.at[:, pl.ds(0, U)], loc.at[0])
    local(w2_in, w2.at[pl.ds(0, 1)], loc.at[1])
    local(bias_in, my_bs.at[0], loc.at[2])
    local(score_in, my_bs.at[1], loc.at[3])
    local(hyp_part, hp.at[0], small_recv.at[2])
    for d in range(1, 4):
        remote(hyp_part, hp.at[SLOT_AT[d]], small_send.at[2], small_recv.at[2], device(x, y, zz(d), c))
    for d in range(4):
        remote(hyp_part, hp.at[4 + SLOT_AT[d]], small_send.at[2], small_recv.at[2], device(x, yy(2), zz(d), c))
    ref_slot = slot_of(mod(z - x + 4, 4))
    for k in range(8):
        dx, dc = k // 2, k % 2
        target = device(xx(dx), ref_y, x, mod(c + dc, 2))
        there = rp.at[ref_j * 4 + ref_slot]
        if k == 0:
            pl.when(ref_self)(lambda: local(ref_part, there, small_recv.at[3]))
            pl.when(jnp.logical_not(ref_self))(
                lambda: remote(ref_part, there, small_send.at[3], small_recv.at[3], target)
            )
        else:
            remote(ref_part, there, small_send.at[3], small_recv.at[3], target)

    def send_bias():
        done(bias_in, loc.at[2])
        done(score_in, loc.at[3])
        local(my_bs, bs.at[hid], small_recv.at[4])
        for d in range(1, 8):
            remote(my_bs, bs.at[hid], small_send.at[4], small_recv.at[4], (blk, mod(hid + d, 8)))

    def forward_z(t):
        two = region(t, quarter, (1, 2))
        done(two, z_recv.at[t])
        send(region(t, quarter, (1, 1), 0), region(t, quarter, (3, 1), 0), z3_recv.at[t], z_down, t)
        send(region(t, quarter, (2, 1), 1), region(t, quarter, (3, 1), 1), z3_recv.at[t], z_up, t)
        for part, target in ((0, x_up), (1, x_down)):
            piece = region(t, quarter, (1, 2), part)
            send(piece, piece, x_recv.at[t], target, t)
        if t + AHEAD < STEPS:
            send_own(t + AHEAD)
        send(two, two, d_recv.at[t], sibling, t)

    def forward_z3(t):
        one = region(t, quarter, (3, 1))
        done(one, z3_recv.at[t])
        for part, target in ((0, x_up), (1, x_down)):
            piece = region(t, quarter, (3, 1), part)
            send(piece, piece, x3_recv.at[t], target, t)
        send(one, one, d3_recv.at[t], sibling, t)

    def forward_x(t):
        two = region(t, quarter_x, (1, 2))
        done(two, x_recv.at[t])
        send(two, two, d_recv.at[t], sibling, t)

    def forward_x3(t):
        one = region(t, quarter_x, (3, 1))
        done(one, x3_recv.at[t])
        send(one, one, d3_recv.at[t], sibling, t)

    def arrived(t):
        if t < STEPS1:
            done(w1.at[pl.ds(0, 2 * Q1), pl.ds(0, 2 * U)], d_recv.at[t])
        else:
            done(w2.at[pl.ds(0, 2), pl.ds(0, 192), pl.ds(0, C2)], d_recv.at[t])

    def arrived3(t):
        if t < STEPS1:
            done(w1.at[pl.ds(0, 2 * Q1), pl.ds(0, U)], d3_recv.at[t])
        else:
            done(w2.at[pl.ds(0, 1), pl.ds(0, 192), pl.ds(0, C2)], d3_recv.at[t])

    def make_feats():
        done(hyp, small_recv.at[0])
        done(ref, small_recv.at[1])
        hypf[...] = hyp[...].astype(F32).reshape(32, 1024)
        right = [ref[j].astype(F32) for j in range(2)]

        def one(h, carry):
            left = hypf[pl.ds(h, 1), :]
            for j in range(2):
                rows = pl.ds(pl.multiple_of(j * 512 + h * 16, 16), 16)
                feats[rows, pl.ds(0, 1024)] = (left * right[j]).astype(BF16)
                feats[rows, pl.ds(1024, 1024)] = jnp.abs(left - right[j]).astype(BF16)
            return carry

        lax.fori_loop(0, 32, one, 0)

    mine = mod(y_hi + y_lo, 2)

    K = 2 * K1
    EARLY = pl.ds(0, 1024)
    LATE = pl.ds(1024, 512)

    def multiply(p, rows, columns):
        value = jnp.dot(feats[rows, pl.ds(p * K, K)], w1[pl.ds(p * K, K), columns], preferred_element_type=F32)
        if p:
            value = acc[rows, columns] + value
        acc[rows, columns] = value

    def block_rows(i):
        slot = 1 - mine if i < 2 else mine
        return slot, pl.multiple_of((i % 2) * 512 + slot * 256, 256)

    def activate(i, columns):
        slot, base = block_rows(i)

        def one(h, carry):
            here = pl.ds(pl.multiple_of(base + h * 16, 16), 16)
            there = pl.ds(pl.multiple_of(i * 256 + h * 16, 16), 16)
            value = acc[here, columns] + hpf[slot, pl.ds(h, 1), columns] + rpf[i % 2, :, columns]
            first[there, columns] = jnp.tanh(value).astype(BF16)
            return carry

        lax.fori_loop(0, 16, one, 0)

    def make_parts():
        done(hp, small_recv.at[2])
        done(rp, small_recv.at[3])
        for s in range(2):
            for g in range(4):
                hpf[s, :, pl.ds(g * U, U)] = hp[s * 4 + g].astype(F32)
                rpf[s, :, pl.ds(g * U, U)] = rp[s * 4 + g].astype(F32)

    def second_weights(n):
        return w2[:, :, pl.ds(n * C2, C2)].reshape(4 * U, C2)

    def theirs(n):
        columns = pl.ds(n * C2, C2)
        for j in range(2):
            value = jnp.dot(first[pl.ds(j * 256, 256), :], second_weights(n), preferred_element_type=F32)
            part_send[j, :, columns] = value.astype(BF16)
            remote(
                part_send.at[j, :, columns], part_recv.at[1 - j, :, columns], small_send.at[5], pr_recv.at[1 - j, n],
                device(x, yy(1) if j == 0 else yy(3), z, c),
            )

    def ours(n):
        for j in range(2):
            part_mine[j, :, pl.ds(n * C2, C2)] = jnp.dot(
                first[pl.ds(512 + j * 256, 256), :], second_weights(n), preferred_element_type=F32
            )

    def finish_second(n):
        columns = pl.ds(n * C2, C2)
        for j in range(2):
            done(part_recv.at[j, :, columns], pr_recv.at[j, n])
            total = jnp.zeros((256, 128), F32) if n == 0 else sacc[j]
            for k in range(C2 // 128):
                g = n * (C2 // 128) + k
                lanes = pl.ds(g * 128, 128)
                value = part_mine[j, :, lanes] + part_recv[j, :, lanes].astype(F32)
                total += jnp.tanh(value + bs[g, 0]) * bs[g, 1]
            sacc[j] = total

    for t in range(STEPS + L3):
        if t < STEPS:
            forward_z(t)
        if 0 <= t - LZ3 < STEPS:
            forward_z3(t - LZ3)
        if 0 <= t - LX < STEPS:
            forward_x(t - LX)
        if 0 <= t - LX3 < STEPS:
            forward_x3(t - LX3)
        if t == 0:
            send_bias()
        if t == 1:
            make_feats()
        if t == 2:
            make_parts()
            done(w1_in, loc.at[0])
            done(w2_in, loc.at[1])
        if 0 <= t - L12 < STEPS:
            arrived(t - L12)
        if 0 <= t - L3 < STEPS:
            arrived3(t - L3)
        a, b = t - L12 - 1, t - L3 - 1
        for i in range(4):
            rows = pl.ds(block_rows(i)[1], 256)
            if 0 <= a < STEPS1 and i // 2 == a % 2:
                multiply(a // 2, rows, EARLY)
                if a // 2 == 3:
                    activate(i, EARLY)
            if 0 <= b < STEPS1 - 2 and i // 2 == b % 2:
                multiply(b // 2, rows, LATE)
        if b == STEPS1 - 2:
            for i in range(4):
                multiply(3, pl.ds(block_rows(i)[1], 256), LATE)
                activate(i, LATE)
        n = t - L3 - STEPS1
        if n >= 0:
            theirs(n)
            ours(n)
    done(bs, small_recv.at[4])
    for n in range(STEPS2):
        finish_second(n)

    lane = lax.broadcasted_iota(jnp.int32, (256, 128), 1)
    row = lax.broadcasted_iota(jnp.int32, (256, 128), 0)
    value = jnp.zeros((16, 128), F32)
    for j in range(2):
        place = z * 32 + mod(yy(4 - j), 2) * 16
        total = jnp.sum(sacc[j], axis=1, keepdims=True)
        total = jnp.where(lane - place == jnp.bitwise_and(row, 15), total, 0.0)
        value += jnp.sum(total.reshape(16, 16, 128), axis=1)
    sm[...] = value

    sc_row = y_hi * 4 + z
    sc_self = mod(y, 2) == y_hi
    for d in range(8):
        target = (mod(y, 2) * 8 + mod(blk, 8), mod(hid + d, 8))
        if d == 0:
            pl.when(sc_self)(lambda: local(sm, sc.at[sc_row], small_recv.at[5]))
            pl.when(jnp.logical_not(sc_self))(
                lambda: remote(sm, sc.at[sc_row], small_send.at[6], small_recv.at[5], target)
            )
        else:
            remote(sm, sc.at[sc_row], small_send.at[6], small_recv.at[5], target)

    done(w1.at[pl.ds(0, 3 * 512), :], w_send.at[0])
    done(w2.at[pl.ds(0, 3)], w_send.at[1])
    done(hyp.at[0], small_send.at[0])
    done(hp.at[pl.ds(0, 7)], small_send.at[2])
    done(bs.at[pl.ds(0, 7)], small_send.at[4])
    done(part_send, small_send.at[5])

    def drain_refs():
        done(rp.at[pl.ds(0, 7)], small_send.at[3])
        done(feats.at[pl.ds(0, 112), pl.ds(0, 1024)], small_send.at[1])

    def drain_others():
        done(rp, small_send.at[3])
        pl.when(x == z)(lambda: done(feats.at[pl.ds(0, 128), pl.ds(0, 1024)], small_send.at[1]))

    pl.when(ref_self)(drain_refs)
    pl.when(jnp.logical_not(ref_self))(drain_others)

    done(sc, small_recv.at[5])
    halves = [sc[4 * k] + sc[4 * k + 1] + sc[4 * k + 2] + sc[4 * k + 3] for k in range(2)]
    lane = lax.broadcasted_iota(jnp.int32, (16, 128), 1)
    row = lax.broadcasted_iota(jnp.int32, (16, 128), 0)
    cross = jnp.bitwise_and(lane, 16) * (1 - y_hi) != 0
    halves = [jnp.where(cross, halves[1 - k], halves[k]) for k in range(2)]
    scores_out[:, pl.ds(0, 128)] = halves[0]
    scores_out[:, pl.ds(128, 128)] = halves[1]
    mean = jnp.sum(halves[0] + halves[1], axis=1, keepdims=True) * (1.0 / 256.0)
    util_out[...] = jnp.sum(jnp.where(lane == row, mean, 0.0), axis=0, keepdims=True)[:, :16]

    pl.when(sc_self)(lambda: done(sc.at[pl.ds(0, 7)], small_send.at[6]))
    pl.when(jnp.logical_not(sc_self))(lambda: done(sc, small_send.at[6]))


def body(hyp_emb, ref_emb, hyp_part, ref_part, pair_weight, out_weight, out_bias, score_weight):
    hbm = pl.BlockSpec(memory_space=pltpu.HBM)
    vmem = pl.BlockSpec(memory_space=pltpu.VMEM)
    dma = pltpu.SemaphoreType.DMA
    scores, utilities = pl.pallas_call(
        kernel,
        out_shape=(jax.ShapeDtypeStruct((16, 256), F32), jax.ShapeDtypeStruct((1, 16), F32)),
        in_specs=[hbm] * 8,
        out_specs=(vmem, vmem),
        scratch_shapes=[
            pltpu.VMEM((2048, 4 * U), BF16),
            pltpu.VMEM((4, U, 1024), BF16),
            pltpu.VMEM((2, 16, 1024), BF16),
            pltpu.VMEM((2, 16, 1024), BF16),
            pltpu.VMEM((8, 16, U), BF16),
            pltpu.VMEM((8, 16, U), BF16),
            pltpu.VMEM((8, 2, 1, 128), F32),
            pltpu.VMEM((2, 1, 128), F32),
            pltpu.VMEM((1024, 2048), BF16),
            pltpu.VMEM((1024, 4 * U), F32),
            pltpu.VMEM((1024, 4 * U), BF16),
            pltpu.VMEM((2, 256, 1024), BF16),
            pltpu.VMEM((2, 256, 1024), BF16),
            pltpu.VMEM((2, 256, 1024), F32),
            pltpu.VMEM((8, 16, 128), F32),
            pltpu.VMEM((16, 128), F32),
            pltpu.VMEM((32, 1024), F32),
            pltpu.VMEM((2, 16, 4 * U), F32),
            pltpu.VMEM((2, 16, 4 * U), F32),
            pltpu.VMEM((2, 256, 128), F32),
            dma((STEPS,)), dma((STEPS,)), dma((STEPS,)), dma((STEPS,)), dma((STEPS,)), dma((STEPS,)),
            dma((2,)), dma((6,)), dma((7,)), dma((4,)), dma((2, STEPS2)),
        ],
        compiler_params=pltpu.CompilerParams(
            collective_id=0, has_side_effects=True, vmem_limit_bytes=60 * 2**20
        ),
        cost_estimate=pl.CostEstimate(flops=9_663_676_416, bytes_accessed=3_000_000, transcendentals=2_097_152),
        name="mbr_scores",
    )(
        hyp_emb, ref_emb, hyp_part, ref_part, pair_weight, out_weight.reshape(1, U, 1024),
        out_bias.reshape(1, 128), score_weight.reshape(1, 128),
    )
    return scores, utilities.reshape(16)


def solution(mesh):
    in_specs = (
        P("blk", None),
        P("blk", None),
        P("blk", "hid"),
        P("blk", "hid"),
        P(None, "hid"),
        P("hid", None),
        P("hid"),
        P("hid"),
    )
    out_specs = (P("blk", None), P("blk"))
    return jax.shard_map(body, mesh=mesh, in_specs=in_specs, out_specs=out_specs, check_vma=False)
```

```python
import functools

import jax
import jax.numpy as jnp
from jax import lax
from jax.experimental import pallas as pl
from jax.experimental.pallas import tpu as pltpu
from jax.sharding import PartitionSpec as P

MESH = pl.DeviceIdType.MESH
BF16 = jnp.bfloat16
F32 = jnp.float32

STEPS1 = 8
STEPS2 = 4
STEPS = STEPS1 + STEPS2
K1 = 2048 // STEPS1
Q1 = K1 // 4
C2 = 1024 // STEPS2
U = 384
AHEAD = 3
LZ3, LX, LX3, L12, L3 = 2, 2, 4, 3, 5


def mod(a, n):
    return lax.rem(a, jnp.int32(n))


def half(a):
    return lax.div(a, jnp.int32(2))


def device(x, y, z, c):
    return ((half(y) * 4 + x) * 2 + c, mod(y, 2) * 4 + z)


def slot_of(rel):
    return rel + half(rel) * (5 - 2 * rel)


SLOT_AT = {0: 0, 1: 2, 2: 3, 3: 1}


def kernel(
    hyp_emb, ref_emb, hyp_part, ref_part, w1_in, w2_in, bias_in, score_in,
    scores_out,
    w1, w2, hyp, ref, hp, rp, bs, my_bs, feats, acc, first, part_send, part_recv, part_mine, sc, sm,
    hypf, hpf, rpf, sacc,
    z_recv, z3_recv, x_recv, x3_recv, d_recv, d3_recv, w_send, small_recv, small_send, loc, pr_recv,
):
    blk = lax.axis_index("blk")
    hid = lax.axis_index("hid")
    c = mod(blk, 2)
    x = mod(half(blk), 4)
    y_hi = lax.div(blk, jnp.int32(8))
    y_lo = lax.div(hid, jnp.int32(4))
    y = y_hi * 2 + y_lo
    z = mod(hid, 4)

    def zz(d):
        return mod(z + d, 4)

    def yy(d):
        return mod(y + d, 4)

    def xx(d):
        return mod(x + d, 4)

    sibling = device(x, y, z, 1 - c)
    z_up, z_down = device(x, y, zz(1), c), device(x, y, zz(3), c)
    x_up, x_down = device(xx(1), y, z, c), device(xx(3), y, z, c)

    ref_j = mod(c + y_lo, 2)
    ref_y = mod(y + 2 * c * (1 - y_lo), 4)
    ref_self = jnp.logical_and(ref_y == y, x == z)

    barrier = pltpu.get_barrier_semaphore()

    def greet(target):
        pl.semaphore_signal(barrier, inc=1, device_id=target, device_id_type=MESH)

    for dy in range(4):
        for dz in range(4):
            if dy or dz:
                greet(device(x, yy(dy), zz(dz), c))
    greet(sibling)
    greet(x_up)
    greet(x_down)
    src_y = half(mod(y + 4 - ref_j, 4)) * 2 + y_lo
    src_self = jnp.logical_and(src_y == y, x == z)
    for dz in range(4):
        source = device(z, src_y, zz(dz), c)
        if dz == 0:
            pl.when(jnp.logical_not(src_self))(functools.partial(greet, source))
        else:
            greet(source)
    pl.semaphore_wait(barrier, 15 + 3 + 4 - jnp.where(ref_self, 1, 0))

    def remote(src, dst, send, recv, target):
        pltpu.make_async_remote_copy(
            src_ref=src, dst_ref=dst, send_sem=send, recv_sem=recv, device_id=target, device_id_type=MESH
        ).start()

    def local(src, dst, sem):
        pltpu.make_async_copy(src, dst, sem).start()

    def done(region, sem):
        pltpu.make_async_copy(region, region, sem).wait()

    quarter = mod(x, 2) * 2 + c
    quarter_x = (1 - mod(x, 2)) * 2 + c

    def region(t, quarter_, slots, part=None):
        lo, n = slots
        size = Q1 if t < STEPS1 else 96
        first_row = quarter_ * size
        if part is not None:
            size //= 2
            first_row += part * size
        if t < STEPS1:
            rows = pl.ds(pl.multiple_of(t * K1 + first_row, size), size)
            return w1.at[rows, pl.ds(lo * U, n * U)]
        rows = pl.ds(pl.multiple_of(first_row, size), size)
        return w2.at[pl.ds(lo, n), rows, pl.ds((t - STEPS1) * C2, C2)]

    def own_piece(t):
        if t < STEPS1:
            rows = pl.ds(pl.multiple_of(t * K1 + quarter * Q1, Q1), Q1)
            return w1_in.at[rows, :]
        rows = pl.ds(pl.multiple_of(quarter * 96, 96), 96)
        return w2_in.at[:, rows, pl.ds((t - STEPS1) * C2, C2)]

    def send(src, dst, recv, target, t):
        remote(src, dst, w_send.at[0 if t < STEPS1 else 1], recv, target)

    def send_own(t):
        send(own_piece(t), region(t, quarter, (1, 1)), z_recv.at[t], z_down, t)
        send(own_piece(t), region(t, quarter, (2, 1)), z_recv.at[t], z_up, t)

    local(hyp_emb, hyp.at[0], small_recv.at[0])
    remote(hyp_emb, hyp.at[1], small_send.at[0], small_recv.at[0], device(x, yy(2), z, c))

    def send_refs():
        for k in range(4):
            target = device(xx(k), ref_y, z, c)
            if k == 0:
                pl.when(ref_self)(lambda: local(ref_emb, ref.at[ref_j], small_recv.at[1]))
                pl.when(jnp.logical_not(ref_self))(
                    lambda: remote(ref_emb, ref.at[ref_j], small_send.at[1], small_recv.at[1], target)
                )
            else:
                remote(ref_emb, ref.at[ref_j], small_send.at[1], small_recv.at[1], target)

    for t in range(AHEAD):
        send_own(t)
    pl.when(x == z)(send_refs)
    local(w1_in, w1.at[:, pl.ds(0, U)], loc.at[0])
    local(w2_in, w2.at[pl.ds(0, 1)], loc.at[1])
    local(bias_in, my_bs.at[0], loc.at[2])
    local(score_in, my_bs.at[1], loc.at[3])
    local(hyp_part, hp.at[0], small_recv.at[2])
    for d in range(1, 4):
        remote(hyp_part, hp.at[SLOT_AT[d]], small_send.at[2], small_recv.at[2], device(x, y, zz(d), c))
    for d in range(4):
        remote(hyp_part, hp.at[4 + SLOT_AT[d]], small_send.at[2], small_recv.at[2], device(x, yy(2), zz(d), c))
    ref_slot = slot_of(mod(z - x + 4, 4))
    for k in range(4):
        target = device(xx(k), ref_y, x, c)
        there = rp.at[ref_j, ref_slot]
        if k == 0:
            pl.when(ref_self)(lambda: local(ref_part, there, small_recv.at[3]))
            pl.when(jnp.logical_not(ref_self))(
                lambda: remote(ref_part, there, small_send.at[3], small_recv.at[3], target)
            )
        else:
            remote(ref_part, there, small_send.at[3], small_recv.at[3], target)

    def hand_refs():
        done(ref.at[ref_j], small_recv.at[1])
        remote(ref.at[ref_j], ref.at[ref_j], small_send.at[7], small_recv.at[6], sibling)

    def hand_ref_parts():
        done(rp.at[ref_j], small_recv.at[3])
        remote(rp.at[ref_j], rp.at[ref_j], small_send.at[8], small_recv.at[7], sibling)

    def send_bias():
        done(bias_in, loc.at[2])
        done(score_in, loc.at[3])
        local(my_bs, bs.at[hid], small_recv.at[4])
        for d in range(1, 8):
            remote(my_bs, bs.at[hid], small_send.at[4], small_recv.at[4], (blk, mod(hid + d, 8)))

    def forward_z(t):
        two = region(t, quarter, (1, 2))
        done(two, z_recv.at[t])
        send(region(t, quarter, (1, 1), 0), region(t, quarter, (3, 1), 0), z3_recv.at[t], z_down, t)
        send(region(t, quarter, (2, 1), 1), region(t, quarter, (3, 1), 1), z3_recv.at[t], z_up, t)
        for part, target in ((0, x_up), (1, x_down)):
            piece = region(t, quarter, (1, 2), part)
            send(piece, piece, x_recv.at[t], target, t)
        if t + AHEAD < STEPS:
            send_own(t + AHEAD)
        send(two, two, d_recv.at[t], sibling, t)

    def forward_z3(t):
        one = region(t, quarter, (3, 1))
        done(one, z3_recv.at[t])
        for part, target in ((0, x_up), (1, x_down)):
            piece = region(t, quarter, (3, 1), part)
            send(piece, piece, x3_recv.at[t], target, t)
        send(one, one, d3_recv.at[t], sibling, t)

    def forward_x(t):
        two = region(t, quarter_x, (1, 2))
        done(two, x_recv.at[t])
        send(two, two, d_recv.at[t], sibling, t)

    def forward_x3(t):
        one = region(t, quarter_x, (3, 1))
        done(one, x3_recv.at[t])
        send(one, one, d3_recv.at[t], sibling, t)

    def arrived(t):
        if t < STEPS1:
            done(w1.at[pl.ds(0, 2 * Q1), pl.ds(0, 2 * U)], d_recv.at[t])
        else:
            done(w2.at[pl.ds(0, 2), pl.ds(0, 192), pl.ds(0, C2)], d_recv.at[t])

    def arrived3(t):
        if t < STEPS1:
            done(w1.at[pl.ds(0, 2 * Q1), pl.ds(0, U)], d3_recv.at[t])
        else:
            done(w2.at[pl.ds(0, 1), pl.ds(0, 192), pl.ds(0, C2)], d3_recv.at[t])

    def make_feats():
        done(hyp, small_recv.at[0])
        done(ref.at[1 - ref_j], small_recv.at[6])
        hypf[...] = hyp[...].astype(F32).reshape(32, 1024)
        right = [ref[j].astype(F32) for j in range(2)]

        def one(h, carry):
            left = hypf[pl.ds(h, 1), :]
            for j in range(2):
                rows = pl.ds(pl.multiple_of(j * 512 + h * 16, 16), 16)
                feats[rows, pl.ds(0, 1024)] = (left * right[j]).astype(BF16)
                feats[rows, pl.ds(1024, 1024)] = jnp.abs(left - right[j]).astype(BF16)
            return carry

        lax.fori_loop(0, 32, one, 0)

    mine = mod(y_hi + y_lo, 2)

    K = 2 * K1
    EARLY = pl.ds(0, 1024)
    LATE = pl.ds(1024, 512)

    def multiply(p, rows, columns):
        value = jnp.dot(feats[rows, pl.ds(p * K, K)], w1[pl.ds(p * K, K), columns], preferred_element_type=F32)
        if p:
            value = acc[rows, columns] + value
        acc[rows, columns] = value

    def block_rows(i):
        slot = 1 - mine if i < 2 else mine
        return slot, pl.multiple_of((i % 2) * 512 + slot * 256, 256)

    def activate(i, columns):
        slot, base = block_rows(i)

        def one(h, carry):
            here = pl.ds(pl.multiple_of(base + h * 16, 16), 16)
            there = pl.ds(pl.multiple_of(i * 256 + h * 16, 16), 16)
            value = acc[here, columns] + hpf[slot, pl.ds(h, 1), columns] + rpf[i % 2, :, columns]
            first[there, columns] = jnp.tanh(value).astype(BF16)
            return carry

        lax.fori_loop(0, 16, one, 0)

    def make_parts():
        done(hp, small_recv.at[2])
        done(rp.at[1 - ref_j], small_recv.at[7])
        for s in range(2):
            for g in range(4):
                hpf[s, :, pl.ds(g * U, U)] = hp[s * 4 + g].astype(F32)
                rpf[s, :, pl.ds(g * U, U)] = rp[s, g].astype(F32)

    def second_weights(n):
        return w2[:, :, pl.ds(n * C2, C2)].reshape(4 * U, C2)

    def theirs(n):
        columns = pl.ds(n * C2, C2)
        for j in range(2):
            value = jnp.dot(first[pl.ds(j * 256, 256), :], second_weights(n), preferred_element_type=F32)
            part_send[j, :, columns] = value.astype(BF16)
            remote(
                part_send.at[j, :, columns], part_recv.at[1 - j, :, columns], small_send.at[5], pr_recv.at[1 - j, n],
                device(x, yy(1) if j == 0 else yy(3), z, c),
            )

    def ours(n):
        for j in range(2):
            part_mine[j, :, pl.ds(n * C2, C2)] = jnp.dot(
                first[pl.ds(512 + j * 256, 256), :], second_weights(n), preferred_element_type=F32
            )

    def finish_second(n):
        columns = pl.ds(n * C2, C2)
        for j in range(2):
            done(part_recv.at[j, :, columns], pr_recv.at[j, n])
            total = jnp.zeros((256, 128), F32) if n == 0 else sacc[j]
            for k in range(C2 // 128):
                g = n * (C2 // 128) + k
                lanes = pl.ds(g * 128, 128)
                value = part_mine[j, :, lanes] + part_recv[j, :, lanes].astype(F32)
                total += jnp.tanh(value + bs[g, 0]) * bs[g, 1]
            sacc[j] = total

    for t in range(STEPS + L3):
        if t < STEPS:
            forward_z(t)
        if 0 <= t - LZ3 < STEPS:
            forward_z3(t - LZ3)
        if 0 <= t - LX < STEPS:
            forward_x(t - LX)
        if 0 <= t - LX3 < STEPS:
            forward_x3(t - LX3)
        if t == 0:
            send_bias()
        if t == 1:
            hand_refs()
            hand_ref_parts()
        if t == 2:
            make_feats()
        if t == 3:
            make_parts()
            done(w1_in, loc.at[0])
            done(w2_in, loc.at[1])
        if 0 <= t - L12 < STEPS:
            arrived(t - L12)
        if 0 <= t - L3 < STEPS:
            arrived3(t - L3)
        a, b = t - L12 - 1, t - L3 - 1
        for i in range(4):
            rows = pl.ds(block_rows(i)[1], 256)
            if 0 <= a < STEPS1 and i // 2 == a % 2:
                multiply(a // 2, rows, EARLY)
                if a // 2 == 3:
                    activate(i, EARLY)
            if 0 <= b < STEPS1 - 2 and i // 2 == b % 2:
                multiply(b // 2, rows, LATE)
        n = t - L3 - STEPS1
        if n >= 0:
            theirs(n)
        for i in range(4):
            if b == STEPS1 - 2 + i // 2:
                multiply(3, pl.ds(block_rows(i)[1], 256), LATE)
                activate(i, LATE)
        if n >= 1:
            ours(n - 1)
    ours(STEPS2 - 1)
    done(bs, small_recv.at[4])
    for n in range(STEPS2):
        finish_second(n)

    lane = lax.broadcasted_iota(jnp.int32, (256, 128), 1)
    row = lax.broadcasted_iota(jnp.int32, (256, 128), 0)
    value = jnp.zeros((16, 128), F32)
    for j in range(2):
        place = z * 32 + mod(yy(4 - j), 2) * 16
        total = jnp.sum(sacc[j], axis=1, keepdims=True) * (1.0 / 256.0)
        total = jnp.where(lane - place == jnp.bitwise_and(row, 15), total, 0.0)
        value += jnp.sum(total.reshape(16, 16, 128), axis=1)
    sm[...] = value

    sc_row = y_hi * 4 + z
    sc_self = mod(y, 2) == y_hi
    for d in range(8):
        target = (mod(y, 2) * 8 + mod(blk, 8), mod(hid + d, 8))
        if d == 0:
            pl.when(sc_self)(lambda: local(sm, sc.at[sc_row], small_recv.at[5]))
            pl.when(jnp.logical_not(sc_self))(
                lambda: remote(sm, sc.at[sc_row], small_send.at[6], small_recv.at[5], target)
            )
        else:
            remote(sm, sc.at[sc_row], small_send.at[6], small_recv.at[5], target)

    done(w1.at[pl.ds(0, 3 * 512), :], w_send.at[0])
    done(w2.at[pl.ds(0, 3)], w_send.at[1])
    done(hyp.at[0], small_send.at[0])
    done(hp.at[pl.ds(0, 7)], small_send.at[2])
    done(bs.at[pl.ds(0, 7)], small_send.at[4])
    done(part_send, small_send.at[5])

    done(ref.at[0], small_send.at[7])
    done(rp.at[0], small_send.at[8])
    pl.when(ref_self)(lambda: done(rp.at[0, pl.ds(0, 3)], small_send.at[3]))
    pl.when(jnp.logical_not(ref_self))(lambda: done(rp.at[0], small_send.at[3]))
    pl.when(ref_self)(lambda: done(feats.at[pl.ds(0, 48), pl.ds(0, 1024)], small_send.at[1]))
    pl.when(jnp.logical_and(x == z, jnp.logical_not(ref_self)))(
        lambda: done(feats.at[pl.ds(0, 64), pl.ds(0, 1024)], small_send.at[1])
    )

    done(sc, small_recv.at[5])
    halves = [sc[4 * k] + sc[4 * k + 1] + sc[4 * k + 2] + sc[4 * k + 3] for k in range(2)]
    lane = lax.broadcasted_iota(jnp.int32, (16, 128), 1)
    cross = jnp.bitwise_and(lane, 16) * (1 - y_hi) != 0
    for k in range(2):
        scores_out[:, pl.ds(k * 128, 128)] = jnp.where(cross, halves[1 - k], halves[k])

    pl.when(sc_self)(lambda: done(sc.at[pl.ds(0, 7)], small_send.at[6]))
    pl.when(jnp.logical_not(sc_self))(lambda: done(sc, small_send.at[6]))


def body(hyp_emb, ref_emb, hyp_part, ref_part, pair_weight, out_weight, out_bias, score_weight):
    hbm = pl.BlockSpec(memory_space=pltpu.HBM)
    vmem = pl.BlockSpec(memory_space=pltpu.VMEM)
    dma = pltpu.SemaphoreType.DMA
    scores = pl.pallas_call(
        kernel,
        out_shape=jax.ShapeDtypeStruct((16, 256), F32),
        in_specs=[hbm] * 8,
        out_specs=vmem,
        scratch_shapes=[
            pltpu.VMEM((2048, 4 * U), BF16),
            pltpu.VMEM((4, U, 1024), BF16),
            pltpu.VMEM((2, 16, 1024), BF16),
            pltpu.VMEM((2, 16, 1024), BF16),
            pltpu.VMEM((8, 16, U), BF16),
            pltpu.VMEM((2, 4, 16, U), BF16),
            pltpu.VMEM((8, 2, 1, 128), F32),
            pltpu.VMEM((2, 1, 128), F32),
            pltpu.VMEM((1024, 2048), BF16),
            pltpu.VMEM((1024, 4 * U), F32),
            pltpu.VMEM((1024, 4 * U), BF16),
            pltpu.VMEM((2, 256, 1024), BF16),
            pltpu.VMEM((2, 256, 1024), BF16),
            pltpu.VMEM((2, 256, 1024), F32),
            pltpu.VMEM((8, 16, 128), F32),
            pltpu.VMEM((16, 128), F32),
            pltpu.VMEM((32, 1024), F32),
            pltpu.VMEM((2, 16, 4 * U), F32),
            pltpu.VMEM((2, 16, 4 * U), F32),
            pltpu.VMEM((2, 256, 128), F32),
            dma((STEPS,)), dma((STEPS,)), dma((STEPS,)), dma((STEPS,)), dma((STEPS,)), dma((STEPS,)),
            dma((2,)), dma((8,)), dma((9,)), dma((4,)), dma((2, STEPS2)),
        ],
        compiler_params=pltpu.CompilerParams(
            collective_id=0, has_side_effects=True, vmem_limit_bytes=60 * 2**20
        ),
        cost_estimate=pl.CostEstimate(flops=9_663_676_416, bytes_accessed=3_000_000, transcendentals=2_097_152),
        name="mbr_scores",
    )(
        hyp_emb, ref_emb, hyp_part, ref_part, pair_weight, out_weight.reshape(1, U, 1024),
        out_bias.reshape(1, 128), score_weight.reshape(1, 128),
    )
    return scores * 256.0, jnp.sum(scores, axis=1)


def solution(mesh):
    in_specs = (
        P("blk", None),
        P("blk", None),
        P("blk", "hid"),
        P("blk", "hid"),
        P(None, "hid"),
        P("hid", None),
        P("hid"),
        P("hid"),
    )
    out_specs = (P("blk", None), P("blk"))
    return jax.shard_map(body, mesh=mesh, in_specs=in_specs, out_specs=out_specs, check_vma=False)
```

```python
import functools

import jax
import jax.numpy as jnp
from jax import lax
from jax.experimental import pallas as pl
from jax.experimental.pallas import tpu as pltpu
from jax.sharding import PartitionSpec as P

MESH = pl.DeviceIdType.MESH
BF16 = jnp.bfloat16
F32 = jnp.float32

STEPS1 = 8
STEPS2 = 4
STEPS = STEPS1 + STEPS2
K1 = 2048 // STEPS1
Q1 = K1 // 4
C2 = 1024 // STEPS2
U = 384
AHEAD = 3
EARLY = 3
LX, LD = 2, 3


def mod(a, n):
    return lax.rem(a, jnp.int32(n))


def half(a):
    return lax.div(a, jnp.int32(2))


def device(x, y, z, c):
    return ((half(y) * 4 + x) * 2 + c, mod(y, 2) * 4 + z)


def slot_of(rel):
    return rel + half(rel) * (5 - 2 * rel)


SLOT_AT = {0: 0, 1: 2, 2: 3, 3: 1}


def kernel(
    hyp_emb, ref_emb, hyp_part, ref_part, w1_in, w2_in, bias_in, score_in,
    scores_out,
    w1, w2, hyp, ref, hp, rp, bs, my_bs, feats, acc, first, part_send, part_recv, part_mine, sc, sm,
    hypf, reff, hpf, rpf, sacc,
    z_recv, z3_recv, y3_recv, x_recv, d_recv, w_send, small_recv, small_send, loc, pr_recv,
):
    blk = lax.axis_index("blk")
    hid = lax.axis_index("hid")
    c = mod(blk, 2)
    x = mod(half(blk), 4)
    y_hi = lax.div(blk, jnp.int32(8))
    y_lo = lax.div(hid, jnp.int32(4))
    y = y_hi * 2 + y_lo
    z = mod(hid, 4)

    def zz(d):
        return mod(z + d, 4)

    def yy(d):
        return mod(y + d, 4)

    def xx(d):
        return mod(x + d, 4)

    sibling = device(x, y, z, 1 - c)
    x_up, x_down = device(xx(1), y, z, c), device(xx(3), y, z, c)
    diagonal_up, diagonal_down = device(x, yy(1), zz(1), c), device(x, yy(3), zz(3), c)
    y_far, z_far = device(x, yy(2), z, c), device(x, y, zz(2), c)

    parity = mod(y_lo + z + c + x, 2)
    to_y, to_z = mod(2 * y_hi + c + parity, 4), x
    to_y2, to_z2 = mod(2 * y_hi + c, 4), xx(1)
    self_a = jnp.logical_and(to_y == y, to_z == z)
    self_b = jnp.logical_and(to_y2 == y, to_z2 == z)
    odd = parity == 1
    block_a = mod(c + y_lo, 2)
    has_b = c == y_lo

    barrier = pltpu.get_barrier_semaphore()

    def greet(target):
        pl.semaphore_signal(barrier, inc=1, device_id=target, device_id_type=MESH)

    for dy in range(4):
        for dz in range(4):
            if dy or dz:
                greet(device(x, yy(dy), zz(dz), c))
    greet(sibling)
    greet(x_up)
    greet(x_down)
    from_hi = half(mod(y + 4 - block_a, 4)) * 2
    for dz in range(4):
        source = device(z, from_hi + mod(y_lo + dz, 2), zz(dz), c)
        if dz == 0:
            pl.when(jnp.logical_not(jnp.logical_and(from_hi + y_lo == y, x == z)))(functools.partial(greet, source))
        else:
            greet(source)

    def greet_b():
        for dz in range(4):
            source = device(zz(3), y_hi * 2 + mod(y_lo + dz, 2), zz(dz), c)
            if dz == 0:
                pl.when(x != zz(3))(functools.partial(greet, source))
            else:
                greet(source)

    pl.when(has_b)(greet_b)
    expected = 15 + 3 + 4 - jnp.where(self_a, 1, 0) + jnp.where(odd, 4, 0) - jnp.where(jnp.logical_and(odd, self_b), 1, 0)
    pl.semaphore_wait(barrier, expected)

    def remote(src, dst, send, recv, target):
        pltpu.make_async_remote_copy(
            src_ref=src, dst_ref=dst, send_sem=send, recv_sem=recv, device_id=target, device_id_type=MESH
        ).start()

    def local(src, dst, sem):
        pltpu.make_async_copy(src, dst, sem).start()

    def done(region, sem):
        pltpu.make_async_copy(region, region, sem).wait()

    quarter = mod(x, 2) * 2 + c
    quarter_x = (1 - mod(x, 2)) * 2 + c

    def region(t, quarter_, slots, part=None):
        lo, n = slots
        size = Q1 if t < STEPS1 else 96
        first_row = quarter_ * size
        if part is not None:
            size //= 2
            first_row += part * size
        if t < STEPS1:
            rows = pl.ds(pl.multiple_of(t * K1 + first_row, size), size)
            return w1.at[rows, pl.ds(lo * U, n * U)]
        rows = pl.ds(pl.multiple_of(first_row, size), size)
        return w2.at[pl.ds(lo, n), rows, pl.ds((t - STEPS1) * C2, C2)]

    def own_piece(t, part=None):
        size = Q1 if t < STEPS1 else 96
        first_row = quarter * size
        if part is not None:
            size //= 2
            first_row += part * size
        if t < STEPS1:
            return w1_in.at[pl.ds(pl.multiple_of(t * K1 + first_row, size), size), :]
        rows = pl.ds(pl.multiple_of(first_row, size), size)
        return w2_in.at[:, rows, pl.ds((t - STEPS1) * C2, C2)]

    def send(src, dst, recv, target, t):
        remote(src, dst, w_send.at[0 if t < STEPS1 else 1], recv, target)

    def send_own(t):
        send(own_piece(t), region(t, quarter, (1, 1)), z_recv.at[t], diagonal_down, t)
        send(own_piece(t), region(t, quarter, (2, 1)), z_recv.at[t], diagonal_up, t)

    def send_own3(t):
        send(own_piece(t, y_hi), region(t, quarter, (3, 1), y_hi), z3_recv.at[t], z_far, t)

    local(hyp_emb, hyp.at[0], small_recv.at[0])
    remote(hyp_emb, hyp.at[1], small_send.at[0], small_recv.at[0], y_far)

    def send_four(src, there, send_sem, recv_sem, target_y, target_z, is_self):
        for k in range(4):
            target = device(xx(k), target_y, target_z, c)
            if k == 0:
                pl.when(is_self)(lambda: local(src, there, recv_sem))
                pl.when(jnp.logical_not(is_self))(lambda: remote(src, there, send_sem, recv_sem, target))
            else:
                remote(src, there, send_sem, recv_sem, target)

    for t in range(AHEAD):
        send_own3(t)
    for t in range(AHEAD):
        send_own(t)
    pl.when(x == z)(
        lambda: send_four(ref_emb, ref.at[parity], small_send.at[1], small_recv.at[1], to_y, to_z, self_a)
    )
    far_b = jnp.logical_and(odd, to_z2 == z)
    pl.when(far_b)(
        lambda: send_four(ref_emb, ref.at[2], small_send.at[10], small_recv.at[8], to_y2, to_z2, self_b)
    )
    local(w1_in, w1.at[:, pl.ds(0, U)], loc.at[0])
    local(w2_in, w2.at[pl.ds(0, 1)], loc.at[1])
    local(bias_in, my_bs.at[0], loc.at[2])
    local(score_in, my_bs.at[1], loc.at[3])
    local(hyp_part, hp.at[0], small_recv.at[2])
    for d in range(4):
        for flip in range(2):
            if d or flip:
                y_there = mod(y_hi + flip, 2) * 2 + mod(y_lo + d, 2)
                remote(
                    hyp_part, hp.at[flip * 4 + SLOT_AT[d]], small_send.at[2], small_recv.at[2],
                    device(x, y_there, zz(d), c),
                )
    slot_a, slot_b = slot_of(mod(z - x + 4, 4)), slot_of(mod(z - x + 3, 4))
    send_four(ref_part, rp.at[parity, slot_a], small_send.at[3], small_recv.at[3], to_y, to_z, self_a)
    pl.when(odd)(
        lambda: send_four(ref_part, rp.at[2, slot_b], small_send.at[9], small_recv.at[9], to_y2, to_z2, self_b)
    )

    def hand(block, direct, sem, other):
        done(block, direct)
        remote(block, block, sem, other, sibling)

    def hand_refs():
        hand(ref.at[block_a], small_recv.at[1], small_send.at[7], small_recv.at[6])
        pl.when(has_b)(lambda: hand(ref.at[2], small_recv.at[8], small_send.at[11], small_recv.at[8]))

    def hand_ref_parts():
        hand(rp.at[block_a], small_recv.at[3], small_send.at[8], small_recv.at[7])
        pl.when(has_b)(lambda: hand(rp.at[2], small_recv.at[9], small_send.at[12], small_recv.at[9]))

    def send_bias():
        done(bias_in, loc.at[2])
        done(score_in, loc.at[3])
        local(my_bs, bs.at[hid], small_recv.at[4])
        for d in range(1, 8):
            remote(my_bs, bs.at[hid], small_send.at[4], small_recv.at[4], (blk, mod(hid + d, 8)))

    def share(t):
        piece = region(t, quarter, (3, 1), y_hi)
        done(piece, z3_recv.at[t])
        send(piece, piece, y3_recv.at[t], y_far, t)
        if t + AHEAD < STEPS:
            send_own3(t + AHEAD)

    def forward_z(t):
        done(region(t, quarter, (1, 2)), z_recv.at[t])
        if t + AHEAD < STEPS:
            send_own(t + AHEAD)
        done(region(t, quarter, (3, 1), 1 - y_hi), y3_recv.at[t])
        for part, target in ((0, x_up), (1, x_down)):
            piece = region(t, quarter, (1, 3), part)
            send(piece, piece, x_recv.at[t], target, t)
        piece = region(t, quarter, (1, 3))
        send(piece, piece, d_recv.at[t], sibling, t)

    def forward_x(t):
        piece = region(t, quarter_x, (1, 3))
        done(piece, x_recv.at[t])
        send(piece, piece, d_recv.at[t], sibling, t)

    def arrived(t):
        if t < STEPS1:
            done(w1.at[pl.ds(0, 2 * Q1), pl.ds(0, 3 * U)], d_recv.at[t])
        else:
            done(w2.at[pl.ds(0, 3), pl.ds(0, 192), pl.ds(0, C2)], d_recv.at[t])

    FIRST_REF = (0, 16, 8, 40)

    def make_feats():
        done(hyp, small_recv.at[0])
        done(ref.at[1 - block_a], small_recv.at[6])
        pl.when(jnp.logical_not(has_b))(lambda: done(ref.at[2], small_recv.at[8]))
        hypf[...] = hyp[...].astype(F32)
        reff[...] = ref[...].astype(F32).reshape(48, 1024)

        def one(r, carry):
            for i in range(4):
                right = reff[pl.ds(FIRST_REF[i] + r, 1), :]
                for s in range(2):
                    left = hypf[s]
                    rows = pl.ds(pl.multiple_of(s * 512 + i * 128 + r * 16, 16), 16)
                    feats[rows, pl.ds(0, 1024)] = (left * right).astype(BF16)
                    feats[rows, pl.ds(1024, 1024)] = jnp.abs(left - right).astype(BF16)
            return carry

        lax.fori_loop(0, 8, one, 0)

    final = mod(y_lo + z, 2)
    mine = mod(y_hi + final, 2)

    K = 2 * K1

    def multiply(p, rows):
        left = feats[rows, pl.ds(p * K, K)]
        for n in range(3):
            columns = pl.ds(n * 512, 512)
            value = jnp.dot(left, w1[pl.ds(p * K, K), columns], preferred_element_type=F32)
            if p:
                value = acc[rows, columns] + value
            acc[rows, columns] = value

    def block_rows(i):
        slot = 1 - mine if i < 2 else mine
        return slot, pl.multiple_of(slot * 512 + (i % 2) * 256, 256)

    def activate(i):
        slot, base = block_rows(i)

        def one(r, carry):
            for j in range(2):
                here = pl.ds(pl.multiple_of(base + j * 128 + r * 16, 16), 16)
                there = pl.ds(pl.multiple_of(i * 256 + j * 128 + r * 16, 16), 16)
                row = FIRST_REF[2 * (i % 2) + j] + r
                value = acc[here, :] + hpf[slot] + rpf[pl.ds(row, 1), :]
                first[there, :] = jnp.tanh(value).astype(BF16)
            return carry

        lax.fori_loop(0, 8, one, 0)

    def make_parts():
        done(hp, small_recv.at[2])
        done(rp.at[1 - block_a], small_recv.at[7])
        pl.when(jnp.logical_not(has_b))(lambda: done(rp.at[2], small_recv.at[9]))
        for g in range(4):
            for s in range(2):
                hpf[s, :, pl.ds(g * U, U)] = hp[s * 4 + g].astype(F32)
            for k in range(3):
                rpf[pl.ds(k * 16, 16), pl.ds(g * U, U)] = rp[k, g].astype(F32)

    def second_weights(n):
        return w2[:, :, pl.ds(n * C2, C2)].reshape(4 * U, C2)

    def theirs(n, blocks=(0, 1)):
        columns = pl.ds(n * C2, C2)
        for j in blocks:
            rows = pl.ds(j * 256, 256)
            value = jnp.dot(first[rows, :], second_weights(n), preferred_element_type=F32)
            part_send[rows, columns] = value.astype(BF16)
            for i in (2 * j, 2 * j + 1):
                target = device(x, (yy(1), yy(3), y, y)[i], (z, z, zz(1), zz(3))[i], c)
                remote(
                    part_send.at[pl.ds(i * 128, 128), columns],
                    part_recv.at[pl.ds((i ^ 1) * 128, 128), columns],
                    small_send.at[5], pr_recv.at[n], target,
                )

    def ours(n):
        for j in range(2):
            rows = pl.ds(j * 256, 256)
            part_mine[rows, pl.ds(n * C2, C2)] = jnp.dot(
                first[pl.ds(512 + j * 256, 256), :], second_weights(n), preferred_element_type=F32
            )

    def finish_second(n):
        columns = pl.ds(n * C2, C2)
        done(part_recv.at[:, columns], pr_recv.at[n])
        for j in range(4):
            rows = pl.ds(j * 128, 128)
            total = jnp.zeros((128, 128), F32) if n == 0 else sacc[rows, :]
            for k in range(C2 // 128):
                g = n * (C2 // 128) + k
                lanes = pl.ds(g * 128, 128)
                value = part_mine[rows, lanes] + part_recv[rows, lanes].astype(F32)
                total += jnp.tanh(value + bs[g, 0]) * bs[g, 1]
            sacc[rows, :] = total

    for t in range(EARLY):
        share(t)
    for t in range(STEPS + LD):
        if t + EARLY < STEPS:
            share(t + EARLY)
        if t < STEPS:
            forward_z(t)
        if 0 <= t - LX < STEPS:
            forward_x(t - LX)
        if t == 0:
            send_bias()
            hand_refs()
            hand_ref_parts()
        if t == 1:
            make_feats()
        if t == 2:
            make_parts()
            done(w1_in, loc.at[0])
            done(w2_in, loc.at[1])
        if 0 <= t - LD < STEPS:
            arrived(t - LD)
        n = t - LD - STEPS1
        a = t - LD - 1
        for i in range(4):
            if 0 <= a < STEPS1 - 2 and i // 2 == a % 2:
                multiply(a // 2, pl.ds(block_rows(i)[1], 256))
            if a == STEPS1 - 2 + i and i < 2:
                multiply(3, pl.ds(block_rows(i)[1], 256))
                activate(i)
        if n == 0:
            theirs(0)
        if n >= 1:
            theirs(n)
            if n < 3:
                multiply(3, pl.ds(block_rows(n + 1)[1], 256))
                activate(n + 1)
    for n in range(STEPS2 - 1):
        ours(n)
    ours(STEPS2 - 1)
    done(bs, small_recv.at[4])
    for n in range(STEPS2):
        finish_second(n)

    lane = lax.broadcasted_iota(jnp.int32, (8, 16, 128), 2)
    row = lax.broadcasted_iota(jnp.int32, (8, 16, 128), 0)
    value = jnp.zeros((16, 128), F32)
    own_place = z * 32 + y_lo * 16
    places = (own_place, z * 32 + (1 - y_lo) * 16, own_place + 8, zz(3) * 32 + y_lo * 16 + 8)
    for i in range(4):
        total = jnp.sum(sacc[pl.ds(i * 128, 128), :].reshape(8, 16, 128), axis=2, keepdims=True) * (1.0 / 256.0)
        value += jnp.sum(jnp.where(lane - places[i] == row, total, 0.0), axis=0)
    sm[...] = value

    sc_row = y_hi * 4 + z
    sc_self = final == y_hi
    for d in range(8):
        target = (final * 8 + mod(blk, 8), mod(hid + d, 8))
        if d == 0:
            pl.when(sc_self)(lambda: local(sm, sc.at[sc_row], small_recv.at[5]))
            pl.when(jnp.logical_not(sc_self))(
                lambda: remote(sm, sc.at[sc_row], small_send.at[6], small_recv.at[5], target)
            )
        else:
            remote(sm, sc.at[sc_row], small_send.at[6], small_recv.at[5], target)

    done(w1.at[pl.ds(0, 3 * 512), :], w_send.at[0])
    done(w2.at[pl.ds(0, 3)], w_send.at[1])
    done(hyp.at[0], small_send.at[0])
    done(hp.at[pl.ds(0, 7)], small_send.at[2])
    done(bs.at[pl.ds(0, 7)], small_send.at[4])
    done(part_send, small_send.at[5])

    done(ref.at[0], small_send.at[7])
    done(rp.at[0], small_send.at[8])

    def drain_b():
        done(ref.at[0], small_send.at[11])
        done(rp.at[0], small_send.at[12])

    pl.when(has_b)(drain_b)

    def drain_four(three, four, sem, is_self):
        pl.when(is_self)(lambda: done(three, sem))
        pl.when(jnp.logical_not(is_self))(lambda: done(four, sem))

    three_embs, four_embs = ref, feats.at[pl.ds(0, 64), pl.ds(0, 1024)]
    three_parts, four_parts = rp.at[0, pl.ds(0, 3)], rp.at[0]
    drain_four(three_parts, four_parts, small_send.at[3], self_a)
    pl.when(odd)(lambda: drain_four(three_parts, four_parts, small_send.at[9], self_b))
    pl.when(x == z)(lambda: drain_four(three_embs, four_embs, small_send.at[1], self_a))
    pl.when(far_b)(lambda: drain_four(three_embs, four_embs, small_send.at[10], self_b))

    done(sc, small_recv.at[5])
    lane = lax.broadcasted_iota(jnp.int32, (16, 128), 1)
    halves = [jnp.zeros((16, 128), F32), jnp.zeros((16, 128), F32)]
    for k in range(4):
        cross = jnp.bitwise_and(lane, 16) * (1 - mod(y_hi + k, 2)) != 0
        low, high = sc[k], sc[4 + k]
        halves[0] += jnp.where(cross, high, low)
        halves[1] += jnp.where(cross, low, high)
    for k in range(2):
        scores_out[:, pl.ds(k * 128, 128)] = halves[k]

    pl.when(sc_self)(lambda: done(sc.at[pl.ds(0, 7)], small_send.at[6]))
    pl.when(jnp.logical_not(sc_self))(lambda: done(sc, small_send.at[6]))


def body(hyp_emb, ref_emb, hyp_part, ref_part, pair_weight, out_weight, out_bias, score_weight):
    hbm = pl.BlockSpec(memory_space=pltpu.HBM)
    vmem = pl.BlockSpec(memory_space=pltpu.VMEM)
    dma = pltpu.SemaphoreType.DMA
    scores = pl.pallas_call(
        kernel,
        out_shape=jax.ShapeDtypeStruct((16, 256), F32),
        in_specs=[hbm] * 8,
        out_specs=vmem,
        scratch_shapes=[
            pltpu.VMEM((2048, 4 * U), BF16),
            pltpu.VMEM((4, U, 1024), BF16),
            pltpu.VMEM((2, 16, 1024), BF16),
            pltpu.VMEM((3, 16, 1024), BF16),
            pltpu.VMEM((8, 16, U), BF16),
            pltpu.VMEM((3, 4, 16, U), BF16),
            pltpu.VMEM((8, 2, 1, 128), F32),
            pltpu.VMEM((2, 1, 128), F32),
            pltpu.VMEM((1024, 2048), BF16),
            pltpu.VMEM((1024, 4 * U), F32),
            pltpu.VMEM((1024, 4 * U), BF16),
            pltpu.VMEM((512, 1024), BF16),
            pltpu.VMEM((512, 1024), BF16),
            pltpu.VMEM((512, 1024), F32),
            pltpu.VMEM((8, 16, 128), F32),
            pltpu.VMEM((16, 128), F32),
            pltpu.VMEM((2, 16, 1024), F32),
            pltpu.VMEM((48, 1024), F32),
            pltpu.VMEM((2, 16, 4 * U), F32),
            pltpu.VMEM((48, 4 * U), F32),
            pltpu.VMEM((512, 128), F32),
            dma((STEPS,)), dma((STEPS,)), dma((STEPS,)), dma((STEPS,)), dma((STEPS,)),
            dma((2,)), dma((10,)), dma((13,)), dma((4,)), dma((STEPS2,)),
        ],
        compiler_params=pltpu.CompilerParams(
            collective_id=0, has_side_effects=True, vmem_limit_bytes=60 * 2**20
        ),
        cost_estimate=pl.CostEstimate(flops=9_663_676_416, bytes_accessed=3_000_000, transcendentals=2_097_152),
        name="mbr_scores",
    )(
        hyp_emb, ref_emb, hyp_part, ref_part, pair_weight, out_weight.reshape(1, U, 1024),
        out_bias.reshape(1, 128), score_weight.reshape(1, 128),
    )
    return scores * 256.0, jnp.sum(scores, axis=1)


def solution(mesh):
    in_specs = (
        P("blk", None),
        P("blk", None),
        P("blk", "hid"),
        P("blk", "hid"),
        P(None, "hid"),
        P("hid", None),
        P("hid"),
        P("hid"),
    )
    out_specs = (P("blk", None), P("blk"))
    return jax.shard_map(body, mesh=mesh, in_specs=in_specs, out_specs=out_specs, check_vma=False)
```

```python
import functools

import jax
import jax.numpy as jnp
from jax import lax
from jax.experimental import pallas as pl
from jax.experimental.pallas import tpu as pltpu
from jax.sharding import PartitionSpec as P

MESH = pl.DeviceIdType.MESH
BF16 = jnp.bfloat16
F32 = jnp.float32

STEPS1 = 8
STEPS2 = 4
STEPS = STEPS1 + STEPS2
K1 = 2048 // STEPS1
Q1 = K1 // 4
C2 = 1024 // STEPS2
U = 384
AHEAD = 3
EARLY = 3
LX, LD = 2, 3


def mod(a, n):
    return lax.rem(a, jnp.int32(n))


def half(a):
    return lax.div(a, jnp.int32(2))


def device(x, y, z, c):
    return ((half(y) * 4 + x) * 2 + c, mod(y, 2) * 4 + z)


def slot_of(rel):
    return rel + half(rel) * (5 - 2 * rel)


SLOT_AT = {0: 0, 1: 2, 2: 3, 3: 1}


def kernel(
    hyp_emb, ref_emb, hyp_part, ref_part, w1_in, w2_in, bias_in, score_in,
    scores_out,
    w1, w2, hyp, ref, hp, rp, bs, my_bs, feats, acc, first, part_send, part_recv, part_mine, sc, sm,
    hypf, reff, hpf, rpf, sacc,
    z_recv, z3_recv, y3_recv, x_recv, d_recv, w_send, small_recv, small_send, loc, pr_recv,
):
    blk = lax.axis_index("blk")
    hid = lax.axis_index("hid")
    c = mod(blk, 2)
    x = mod(half(blk), 4)
    y_hi = lax.div(blk, jnp.int32(8))
    y_lo = lax.div(hid, jnp.int32(4))
    y = y_hi * 2 + y_lo
    z = mod(hid, 4)

    def zz(d):
        return mod(z + d, 4)

    def yy(d):
        return mod(y + d, 4)

    def xx(d):
        return mod(x + d, 4)

    sibling = device(x, y, z, 1 - c)
    x_up, x_down = device(xx(1), y, z, c), device(xx(3), y, z, c)
    diagonal_up, diagonal_down = device(x, yy(1), zz(1), c), device(x, yy(3), zz(3), c)
    y_far, z_far = device(x, yy(2), z, c), device(x, y, zz(2), c)

    parity = mod(y_lo + z + c + x, 2)
    to_y, to_z = mod(2 * y_hi + c + parity, 4), x
    to_y2, to_z2 = mod(2 * y_hi + c, 4), xx(1)
    self_a = jnp.logical_and(to_y == y, to_z == z)
    self_b = jnp.logical_and(to_y2 == y, to_z2 == z)
    odd = parity == 1
    block_a = mod(c + y_lo, 2)
    has_b = c == y_lo

    barrier = pltpu.get_barrier_semaphore()

    def greet(target):
        pl.semaphore_signal(barrier, inc=1, device_id=target, device_id_type=MESH)

    for dy in range(4):
        for dz in range(4):
            if dy or dz:
                greet(device(x, yy(dy), zz(dz), c))
    greet(sibling)
    greet(x_up)
    greet(x_down)
    from_hi = half(mod(y + 4 - block_a, 4)) * 2
    for dz in range(4):
        source = device(z, from_hi + mod(y_lo + dz, 2), zz(dz), c)
        if dz == 0:
            pl.when(jnp.logical_not(jnp.logical_and(from_hi + y_lo == y, x == z)))(functools.partial(greet, source))
        else:
            greet(source)

    def greet_b():
        for dz in range(4):
            source = device(zz(3), y_hi * 2 + mod(y_lo + dz, 2), zz(dz), c)
            if dz == 0:
                pl.when(x != zz(3))(functools.partial(greet, source))
            else:
                greet(source)

    pl.when(has_b)(greet_b)
    expected = 15 + 3 + 4 - jnp.where(self_a, 1, 0) + jnp.where(odd, 4, 0) - jnp.where(jnp.logical_and(odd, self_b), 1, 0)
    pl.semaphore_wait(barrier, expected)

    def remote(src, dst, send, recv, target):
        pltpu.make_async_remote_copy(
            src_ref=src, dst_ref=dst, send_sem=send, recv_sem=recv, device_id=target, device_id_type=MESH
        ).start()

    def local(src, dst, sem):
        pltpu.make_async_copy(src, dst, sem).start()

    def done(region, sem):
        pltpu.make_async_copy(region, region, sem).wait()

    quarter = mod(x, 2) * 2 + c
    quarter_x = (1 - mod(x, 2)) * 2 + c

    def region(t, quarter_, slots, part=None):
        lo, n = slots
        size = Q1 if t < STEPS1 else 96
        first_row = quarter_ * size
        if part is not None:
            size //= 2
            first_row += part * size
        if t < STEPS1:
            rows = pl.ds(pl.multiple_of(t * K1 + first_row, size), size)
            return w1.at[rows, pl.ds(lo * U, n * U)]
        rows = pl.ds(pl.multiple_of(first_row, size), size)
        return w2.at[pl.ds(lo, n), rows, pl.ds((t - STEPS1) * C2, C2)]

    def own_piece(t, part=None):
        size = Q1 if t < STEPS1 else 96
        first_row = quarter * size
        if part is not None:
            size //= 2
            first_row += part * size
        if t < STEPS1:
            return w1_in.at[pl.ds(pl.multiple_of(t * K1 + first_row, size), size), :]
        rows = pl.ds(pl.multiple_of(first_row, size), size)
        return w2_in.at[:, rows, pl.ds((t - STEPS1) * C2, C2)]

    def send(src, dst, recv, target, t):
        remote(src, dst, w_send.at[0 if t < STEPS1 else 1], recv, target)

    def send_own(t):
        send(own_piece(t), region(t, quarter, (1, 1)), z_recv.at[t], diagonal_down, t)
        send(own_piece(t), region(t, quarter, (2, 1)), z_recv.at[t], diagonal_up, t)

    def send_own3(t):
        send(own_piece(t, y_hi), region(t, quarter, (3, 1), y_hi), z3_recv.at[t], z_far, t)

    local(hyp_emb, hyp.at[0], small_recv.at[0])
    remote(hyp_emb, hyp.at[1], small_send.at[0], small_recv.at[0], y_far)

    def send_four(src, there, send_sem, recv_sem, target_y, target_z, is_self):
        for k in range(4):
            target = device(xx(k), target_y, target_z, c)
            if k == 0:
                pl.when(is_self)(lambda: local(src, there, recv_sem))
                pl.when(jnp.logical_not(is_self))(lambda: remote(src, there, send_sem, recv_sem, target))
            else:
                remote(src, there, send_sem, recv_sem, target)

    for t in range(AHEAD):
        send_own3(t)
    for t in range(AHEAD):
        send_own(t)
    pl.when(x == z)(
        lambda: send_four(ref_emb, ref.at[parity], small_send.at[1], small_recv.at[1], to_y, to_z, self_a)
    )
    far_b = jnp.logical_and(odd, to_z2 == z)
    pl.when(far_b)(
        lambda: send_four(ref_emb, ref.at[2], small_send.at[10], small_recv.at[8], to_y2, to_z2, self_b)
    )
    local(w1_in, w1.at[:, pl.ds(0, U)], loc.at[0])
    local(w2_in, w2.at[pl.ds(0, 1)], loc.at[1])
    local(bias_in, my_bs.at[0], loc.at[2])
    local(score_in, my_bs.at[1], loc.at[3])
    local(hyp_part, hp.at[0], small_recv.at[2])
    for d in range(4):
        for flip in range(2):
            if d or flip:
                y_there = mod(y_hi + flip, 2) * 2 + mod(y_lo + d, 2)
                remote(
                    hyp_part, hp.at[flip * 4 + SLOT_AT[d]], small_send.at[2], small_recv.at[2],
                    device(x, y_there, zz(d), c),
                )
    slot_a, slot_b = slot_of(mod(z - x + 4, 4)), slot_of(mod(z - x + 3, 4))
    send_four(ref_part, rp.at[parity, slot_a], small_send.at[3], small_recv.at[3], to_y, to_z, self_a)
    pl.when(odd)(
        lambda: send_four(ref_part, rp.at[2, slot_b], small_send.at[9], small_recv.at[9], to_y2, to_z2, self_b)
    )

    def hand(block, direct, sem, other):
        done(block, direct)
        remote(block, block, sem, other, sibling)

    def hand_refs():
        hand(ref.at[block_a], small_recv.at[1], small_send.at[7], small_recv.at[6])
        pl.when(has_b)(lambda: hand(ref.at[2], small_recv.at[8], small_send.at[11], small_recv.at[8]))

    def hand_ref_parts():
        hand(rp.at[block_a], small_recv.at[3], small_send.at[8], small_recv.at[7])
        pl.when(has_b)(lambda: hand(rp.at[2], small_recv.at[9], small_send.at[12], small_recv.at[9]))

    def send_bias():
        done(bias_in, loc.at[2])
        done(score_in, loc.at[3])
        local(my_bs, bs.at[hid], small_recv.at[4])
        for d in range(1, 8):
            remote(my_bs, bs.at[hid], small_send.at[4], small_recv.at[4], (blk, mod(hid + d, 8)))

    def share(t):
        piece = region(t, quarter, (3, 1), y_hi)
        done(piece, z3_recv.at[t])
        send(piece, piece, y3_recv.at[t], y_far, t)
        if t + AHEAD < STEPS:
            send_own3(t + AHEAD)

    def forward_z(t):
        done(region(t, quarter, (1, 2)), z_recv.at[t])
        if t + AHEAD < STEPS:
            send_own(t + AHEAD)
        done(region(t, quarter, (3, 1), 1 - y_hi), y3_recv.at[t])
        for part, target in ((0, x_up), (1, x_down)):
            piece = region(t, quarter, (1, 3), part)
            send(piece, piece, x_recv.at[t], target, t)
        piece = region(t, quarter, (1, 3))
        send(piece, piece, d_recv.at[t], sibling, t)

    def forward_x(t):
        piece = region(t, quarter_x, (1, 3))
        done(piece, x_recv.at[t])
        send(piece, piece, d_recv.at[t], sibling, t)

    def arrived(t):
        if t < STEPS1:
            done(w1.at[pl.ds(0, 2 * Q1), pl.ds(0, 3 * U)], d_recv.at[t])
        else:
            done(w2.at[pl.ds(0, 3), pl.ds(0, 192), pl.ds(0, C2)], d_recv.at[t])

    FIRST_REF = (0, 16, 8, 40)

    def make_feats():
        done(hyp, small_recv.at[0])
        done(ref.at[1 - block_a], small_recv.at[6])
        pl.when(jnp.logical_not(has_b))(lambda: done(ref.at[2], small_recv.at[8]))
        hypf[...] = hyp[...].astype(F32)
        reff[...] = ref[...].astype(F32).reshape(48, 1024)

        def one(r, carry):
            for i in range(4):
                right = reff[pl.ds(FIRST_REF[i] + r, 1), :]
                for s in range(2):
                    left = hypf[s]
                    rows = pl.ds(pl.multiple_of(s * 512 + i * 128 + r * 16, 16), 16)
                    feats[rows, pl.ds(0, 1024)] = (left * right).astype(BF16)
                    feats[rows, pl.ds(1024, 1024)] = jnp.abs(left - right).astype(BF16)
            return carry

        lax.fori_loop(0, 8, one, 0)

    final = mod(y_lo + z, 2)
    mine = mod(y_hi + final, 2)

    K = 2 * K1

    def multiply(p, rows):
        left = feats[rows, pl.ds(p * K, K)]
        value = jnp.dot(left, w1[pl.ds(p * K, K), :], preferred_element_type=F32)
        if p:
            value = acc[rows, :] + value
        acc[rows, :] = value

    def block_rows(i):
        slot = 1 - mine if i < 2 else mine
        return slot, pl.multiple_of(slot * 512 + (i % 2) * 256, 256)

    def activate(i):
        slot, base = block_rows(i)

        def one(r, carry):
            for j in range(2):
                here = pl.ds(pl.multiple_of(base + j * 128 + r * 16, 16), 16)
                there = pl.ds(pl.multiple_of(i * 256 + j * 128 + r * 16, 16), 16)
                row = FIRST_REF[2 * (i % 2) + j] + r
                value = acc[here, :] + hpf[slot] + rpf[pl.ds(row, 1), :]
                first[there, :] = jnp.tanh(value).astype(BF16)
            return carry

        lax.fori_loop(0, 8, one, 0)

    def make_parts():
        done(hp, small_recv.at[2])
        done(rp.at[1 - block_a], small_recv.at[7])
        pl.when(jnp.logical_not(has_b))(lambda: done(rp.at[2], small_recv.at[9]))
        for g in range(4):
            for s in range(2):
                hpf[s, :, pl.ds(g * U, U)] = hp[s * 4 + g].astype(F32)
            for k in range(3):
                rpf[pl.ds(k * 16, 16), pl.ds(g * U, U)] = rp[k, g].astype(F32)

    def second_weights(n):
        return w2[:, :, pl.ds(n * C2, C2)].reshape(4 * U, C2)

    def theirs(n, blocks=(0, 1)):
        columns = pl.ds(n * C2, C2)
        for j in blocks:
            rows = pl.ds(j * 256, 256)
            value = jnp.dot(first[rows, :], second_weights(n), preferred_element_type=F32)
            part_send[rows, columns] = value.astype(BF16)
            for i in (2 * j, 2 * j + 1):
                target = device(x, (yy(1), yy(3), y, y)[i], (z, z, zz(1), zz(3))[i], c)
                remote(
                    part_send.at[pl.ds(i * 128, 128), columns],
                    part_recv.at[pl.ds((i ^ 1) * 128, 128), columns],
                    small_send.at[5], pr_recv.at[n], target,
                )

    def ours(n):
        for j in range(2):
            rows = pl.ds(j * 256, 256)
            part_mine[rows, pl.ds(n * C2, C2)] = jnp.dot(
                first[pl.ds(512 + j * 256, 256), :], second_weights(n), preferred_element_type=F32
            )

    def finish_second(n):
        columns = pl.ds(n * C2, C2)
        done(part_recv.at[:, columns], pr_recv.at[n])
        for j in range(4):
            rows = pl.ds(j * 128, 128)
            total = jnp.zeros((128, 128), F32) if n == 0 else sacc[rows, :]
            for k in range(C2 // 128):
                g = n * (C2 // 128) + k
                lanes = pl.ds(g * 128, 128)
                value = part_mine[rows, lanes] + part_recv[rows, lanes].astype(F32)
                total += jnp.tanh(value + bs[g, 0]) * bs[g, 1]
            sacc[rows, :] = total

    for t in range(EARLY):
        share(t)
    for t in range(STEPS + LD):
        if t + EARLY < STEPS:
            share(t + EARLY)
        if t < STEPS:
            forward_z(t)
        if 0 <= t - LX < STEPS:
            forward_x(t - LX)
        if t == 0:
            send_bias()
            hand_refs()
            hand_ref_parts()
        if t == 1:
            make_feats()
        if t == 2:
            make_parts()
            done(w1_in, loc.at[0])
            done(w2_in, loc.at[1])
        if 0 <= t - LD < STEPS:
            arrived(t - LD)
        n = t - LD - STEPS1
        a = t - LD - 1
        if n == 0:
            theirs(0, (0,))
        for i in range(4):
            if 0 <= a < STEPS1 - 2 and i // 2 == a % 2:
                multiply(a // 2, pl.ds(block_rows(i)[1], 256))
            if a == STEPS1 - 2 + i and i < 2:
                multiply(3, pl.ds(block_rows(i)[1], 256))
                activate(i)
        if n == 0:
            theirs(0, (1,))
        if n >= 1:
            theirs(n)
            if n < 3:
                multiply(3, pl.ds(block_rows(n + 1)[1], 256))
                activate(n + 1)
    for n in range(STEPS2 - 1):
        ours(n)
    ours(STEPS2 - 1)
    done(bs, small_recv.at[4])
    for n in range(STEPS2):
        finish_second(n)

    lane = lax.broadcasted_iota(jnp.int32, (8, 16, 128), 2)
    row = lax.broadcasted_iota(jnp.int32, (8, 16, 128), 0)
    value = jnp.zeros((16, 128), F32)
    own_place = z * 32 + y_lo * 16
    places = (own_place, z * 32 + (1 - y_lo) * 16, own_place + 8, zz(3) * 32 + y_lo * 16 + 8)
    for i in range(4):
        total = jnp.sum(sacc[pl.ds(i * 128, 128), :].reshape(8, 16, 128), axis=2, keepdims=True) * (1.0 / 256.0)
        value += jnp.sum(jnp.where(lane - places[i] == row, total, 0.0), axis=0)
    sm[...] = value

    sc_row = y_hi * 4 + z
    sc_self = final == y_hi
    for d in range(8):
        target = (final * 8 + mod(blk, 8), mod(hid + d, 8))
        if d == 0:
            pl.when(sc_self)(lambda: local(sm, sc.at[sc_row], small_recv.at[5]))
            pl.when(jnp.logical_not(sc_self))(
                lambda: remote(sm, sc.at[sc_row], small_send.at[6], small_recv.at[5], target)
            )
        else:
            remote(sm, sc.at[sc_row], small_send.at[6], small_recv.at[5], target)

    done(w1.at[pl.ds(0, 3 * 512), :], w_send.at[0])
    done(w2.at[pl.ds(0, 3)], w_send.at[1])
    done(hyp.at[0], small_send.at[0])
    done(hp.at[pl.ds(0, 7)], small_send.at[2])
    done(bs.at[pl.ds(0, 7)], small_send.at[4])
    done(part_send, small_send.at[5])

    done(ref.at[0], small_send.at[7])
    done(rp.at[0], small_send.at[8])

    def drain_b():
        done(ref.at[0], small_send.at[11])
        done(rp.at[0], small_send.at[12])

    pl.when(has_b)(drain_b)

    def drain_four(three, four, sem, is_self):
        pl.when(is_self)(lambda: done(three, sem))
        pl.when(jnp.logical_not(is_self))(lambda: done(four, sem))

    three_embs, four_embs = ref, feats.at[pl.ds(0, 64), pl.ds(0, 1024)]
    three_parts, four_parts = rp.at[0, pl.ds(0, 3)], rp.at[0]
    drain_four(three_parts, four_parts, small_send.at[3], self_a)
    pl.when(odd)(lambda: drain_four(three_parts, four_parts, small_send.at[9], self_b))
    pl.when(x == z)(lambda: drain_four(three_embs, four_embs, small_send.at[1], self_a))
    pl.when(far_b)(lambda: drain_four(three_embs, four_embs, small_send.at[10], self_b))

    done(sc, small_recv.at[5])
    lane = lax.broadcasted_iota(jnp.int32, (16, 128), 1)
    halves = [jnp.zeros((16, 128), F32), jnp.zeros((16, 128), F32)]
    for k in range(4):
        cross = jnp.bitwise_and(lane, 16) * (1 - mod(y_hi + k, 2)) != 0
        low, high = sc[k], sc[4 + k]
        halves[0] += jnp.where(cross, high, low)
        halves[1] += jnp.where(cross, low, high)
    for k in range(2):
        scores_out[:, pl.ds(k * 128, 128)] = halves[k]

    pl.when(sc_self)(lambda: done(sc.at[pl.ds(0, 7)], small_send.at[6]))
    pl.when(jnp.logical_not(sc_self))(lambda: done(sc, small_send.at[6]))


def body(hyp_emb, ref_emb, hyp_part, ref_part, pair_weight, out_weight, out_bias, score_weight):
    hbm = pl.BlockSpec(memory_space=pltpu.HBM)
    vmem = pl.BlockSpec(memory_space=pltpu.VMEM)
    dma = pltpu.SemaphoreType.DMA
    scores = pl.pallas_call(
        kernel,
        out_shape=jax.ShapeDtypeStruct((16, 256), F32),
        in_specs=[hbm] * 8,
        out_specs=vmem,
        scratch_shapes=[
            pltpu.VMEM((2048, 4 * U), BF16),
            pltpu.VMEM((4, U, 1024), BF16),
            pltpu.VMEM((2, 16, 1024), BF16),
            pltpu.VMEM((3, 16, 1024), BF16),
            pltpu.VMEM((8, 16, U), BF16),
            pltpu.VMEM((3, 4, 16, U), BF16),
            pltpu.VMEM((8, 2, 1, 128), F32),
            pltpu.VMEM((2, 1, 128), F32),
            pltpu.VMEM((1024, 2048), BF16),
            pltpu.VMEM((1024, 4 * U), F32),
            pltpu.VMEM((1024, 4 * U), BF16),
            pltpu.VMEM((512, 1024), BF16),
            pltpu.VMEM((512, 1024), BF16),
            pltpu.VMEM((512, 1024), F32),
            pltpu.VMEM((8, 16, 128), F32),
            pltpu.VMEM((16, 128), F32),
            pltpu.VMEM((2, 16, 1024), F32),
            pltpu.VMEM((48, 1024), F32),
            pltpu.VMEM((2, 16, 4 * U), F32),
            pltpu.VMEM((48, 4 * U), F32),
            pltpu.VMEM((512, 128), F32),
            dma((STEPS,)), dma((STEPS,)), dma((STEPS,)), dma((STEPS,)), dma((STEPS,)),
            dma((2,)), dma((10,)), dma((13,)), dma((4,)), dma((STEPS2,)),
        ],
        compiler_params=pltpu.CompilerParams(
            collective_id=0, has_side_effects=True, vmem_limit_bytes=60 * 2**20
        ),
        cost_estimate=pl.CostEstimate(flops=9_663_676_416, bytes_accessed=3_000_000, transcendentals=2_097_152),
        name="mbr_scores",
    )(
        hyp_emb, ref_emb, hyp_part, ref_part, pair_weight, out_weight.reshape(1, U, 1024),
        out_bias.reshape(1, 128), score_weight.reshape(1, 128),
    )
    return scores * 256.0, jnp.sum(scores, axis=1)


def solution(mesh):
    in_specs = (
        P("blk", None),
        P("blk", None),
        P("blk", "hid"),
        P("blk", "hid"),
        P(None, "hid"),
        P("hid", None),
        P("hid"),
        P("hid"),
    )
    out_specs = (P("blk", None), P("blk"))
    return jax.shard_map(body, mesh=mesh, in_specs=in_specs, out_specs=out_specs, check_vma=False)
```
